32 devices in a mesh: groups: 2 (over x), wide: 16 (over z, y, core).
Axes of the slice: x: 2, y: 2, z: 4, core: 2. Of those that a mesh axis runs over, the one named last changes fastest.
Arguments:
- frames: bfloat16 [2048, 3072], P(('groups', 'wide')), parts along dimension 0, may hold values from -6 to 6
- latent_len: int32 [64], P('groups'), parts along dimension 0, may hold values from 1 to 9, as said below
- reader: int32 [64], P('groups'), parts along dimension 0, may hold values from 0 to 15, as said below
- owner: int32 [64], P('groups'), parts along dimension 0, may hold values from 0 to 15, as said below
- w_in: bfloat16 [128, 81], replicated, may hold values from -0.625 to 0.625
- b_in: float32 [128], replicated, may hold values from -3 to 3
- g_in: float32 [128], replicated, may hold values from 0.25 to 1.75
- w_down: bfloat16 [128, 512], replicated, may hold values from -0.25 to 0.25
- b_down: float32 [128], replicated, may hold values from -3 to 3
- g_down: float32 [128], replicated, may hold values from 0.25 to 1.75
- w_head: bfloat16 [16, 8192], replicated, may hold values from -0.0625 to 0.0625
- b_head: float32 [16], replicated, may hold values from -3 to 3
Outputs:
- latents: bfloat16 [576, 256], P(('groups', 'wide')), parts along dimension 0
The draws below stay inside these ranges and needn't reach their ends.
There are 2 independent parts, one for each index of `groups`. The reference program is written for one: setup_inputs(seed, part) draws one part's arguments, and reference() takes and returns one part's arrays. A program takes and returns all parts, laid end to end along the dimension named above; an argument that names none is the same for every part. Nothing has to cross between parts.
Inputs may be any that keep to these rules, and one draw needn't show every extreme that they name: `latent_len`: all entries sum to 144. Every reader holds exactly two clips, with at most 16 latent frames between them; some reader holds exactly 16. An owner holds at most four clips and at most 18 latent frames; some owner holds four clips with 18 latent frames.
All inputs are finite; a program needn't handle non-finite values.
Results may differ from the reference program's by a relative error of at most 0.0046.
Values may be sent and summed in bfloat16 or wider, within the bound.
A program may use at most 256 MiB of HBM per device.

```python
import jax
import jax.numpy as jnp
from jax import lax

C = 128
LAT = 16
LR = 4
GROUP_DEV = 9
PIX = 32
READ_F = 64
OWN_G = 18
GROUPS = 144
N_WIDE = 16


def plan_draw(key):
    wide_n = N_WIDE
    pair_count = wide_n // 2
    key_list = jax.random.split(jax.random.fold_in(key, 11), 7)
    tilt_by = jax.random.randint(key_list[0], (pair_count,), 0, GROUP_DEV - 2)
    forced = jax.random.randint(key_list[1], (), 0, pair_count)
    pair_ids = jnp.arange(pair_count)
    tilt_by = jnp.where(pair_ids == forced, GROUP_DEV - 2, tilt_by)
    totals = jnp.stack([GROUP_DEV + tilt_by, GROUP_DEV - tilt_by], axis=1).reshape(wide_n)
    low_len = jnp.maximum(1, totals - GROUP_DEV)
    high_len = jnp.minimum(GROUP_DEV, totals - 1)
    spread_draw = jax.random.randint(key_list[2], (wide_n,), 0, 1000)
    first_len = low_len + spread_draw % (high_len - low_len + 1)
    heavy_reader = jnp.arange(wide_n) == 2 * forced
    first_len = jnp.where(heavy_reader, high_len, first_len)
    slot_len = jnp.stack([first_len, totals - first_len], axis=1).reshape(2 * wide_n)
    reader_perm = jax.random.permutation(key_list[3], wide_n)
    clip_perm = jax.random.permutation(key_list[4], 2 * wide_n)
    owner_perm = jax.random.permutation(key_list[5], wide_n)
    slot_ids = jnp.arange(2 * wide_n)
    slot_reader = reader_perm[slot_ids // 2]
    owner_pick = jax.random.randint(key_list[6], (2 * wide_n,), 0, 2)
    owner_pick = jnp.where(slot_ids // 4 == forced, 0, owner_pick)
    slot_owner = owner_perm[2 * (slot_ids // 4) + owner_pick]
    latent_len = jnp.zeros((2 * wide_n,), jnp.int32).at[clip_perm].set(slot_len.astype(jnp.int32))
    reader = jnp.zeros((2 * wide_n,), jnp.int32).at[clip_perm].set(slot_reader.astype(jnp.int32))
    owner = jnp.zeros((2 * wide_n,), jnp.int32).at[clip_perm].set(slot_owner.astype(jnp.int32))
    return (latent_len, reader, owner)


def draw_latent_len(key, part):
    return plan_draw(key)[0]


def draw_reader(key, part):
    return plan_draw(key)[1]


def draw_owner(key, part):
    return plan_draw(key)[2]


def shard_levels(stream_key, shape, cuts, least, largest):
    level = 1.0
    for axis_at, shards_of in cuts:
        heights = jax.random.uniform(jax.random.fold_in(jax.random.fold_in(stream_key, 6), axis_at), (shards_of,), jnp.float32, least / len(cuts), largest / len(cuts))
        level = level * jnp.repeat(jnp.exp(heights), shape[axis_at] // shards_of).reshape((-1,) + (1,) * (len(shape) - 1 - axis_at))
    return level


def scatter_about(own_key, dims, scale, most, shards=(), kind=jnp.bfloat16):
    loudness = shard_levels(own_key, dims, shards, -0.22, 0.18) if shards else 1.0
    entries = jax.random.normal(own_key, dims, jnp.float32) * scale * loudness
    return jnp.minimum(jnp.maximum(entries, -most), most).astype(kind)


def setup_inputs(seed: int = 0, part: int = 0) -> dict:
    streams_of = jax.random.split(jax.random.key(seed), 13)
    own_keys = jax.random.split(jax.random.fold_in(streams_of[12], part), 13)
    frames = scatter_about(own_keys[0], (N_WIDE * READ_F, 3 * PIX * PIX), 1.0, 6.0, ((0, 16),))
    latent_len = draw_latent_len(jax.random.fold_in(jax.random.fold_in(streams_of[12], part), 71), part)
    reader = draw_reader(jax.random.fold_in(jax.random.fold_in(streams_of[12], part), 71), part)
    owner = draw_owner(jax.random.fold_in(jax.random.fold_in(streams_of[12], part), 71), part)
    w_in = scatter_about(streams_of[4], (C, 81), 81 ** -0.5, 0.625)
    b_in = scatter_about(streams_of[5], (C,), 0.5, 3.0, (), jnp.float32)
    g_in = jnp.clip(1.0 + 0.15 * jax.random.normal(streams_of[6], (C,), jnp.float32), 0.25, 1.75)
    w_down = scatter_about(streams_of[7], (C, 4 * C), (4 * C) ** -0.5, 0.25)
    b_down = scatter_about(streams_of[8], (C,), 0.5, 3.0, (), jnp.float32)
    g_down = jnp.clip(1.0 + 0.15 * jax.random.normal(streams_of[9], (C,), jnp.float32), 0.25, 1.75)
    w_head = scatter_about(streams_of[10], (LAT, 64 * C), (64 * C) ** -0.5, 0.0625)
    b_head = scatter_about(streams_of[11], (LAT,), 0.5, 3.0, (), jnp.float32)
    return dict(frames=frames, latent_len=latent_len, reader=reader, owner=owner, w_in=w_in, b_in=b_in, g_in=g_in, w_down=w_down, b_down=b_down, g_down=g_down, w_head=w_head, b_head=b_head)


epsilon = 1e-06

def clip_tables(latent_len, reader, owner):
    clip_count = latent_len.shape[0]
    clip_range = jnp.arange(clip_count, dtype=jnp.int32)
    earlier = clip_range[None, :] < clip_range[:, None]
    frame_len = 4 * latent_len - 3
    same_reader = reader[None, :] == reader[:, None]
    same_owner = owner[None, :] == owner[:, None]
    read_off = lax.optimization_barrier(jnp.sum(jnp.where(earlier & same_reader, frame_len[None, :], 0), axis=1)).astype(jnp.int32)
    own_off = lax.optimization_barrier(jnp.sum(jnp.where(earlier & same_owner, latent_len[None, :], 0), axis=1)).astype(jnp.int32)
    order_key = reader * clip_count + clip_range
    before = order_key[None, :] < order_key[:, None]
    deal_start = lax.optimization_barrier(jnp.sum(jnp.where(before, latent_len[None, :], 0), axis=1)).astype(jnp.int32)
    return (read_off, own_off, deal_start)

def find_clip(group_ids, deal_start, latent_len):
    clip_range = jnp.arange(latent_len.shape[0], dtype=jnp.int32)
    inside = (deal_start[None, :] <= group_ids[:, None]) & (group_ids[:, None] < (deal_start + latent_len)[None, :])
    clip_ids = lax.optimization_barrier(jnp.sum(jnp.where(inside, clip_range[None, :], 0), axis=1)).astype(jnp.int32)
    present = jnp.any(inside, axis=1)
    latent_idx = (group_ids - deal_start[clip_ids]).astype(jnp.int32)
    return (clip_ids, latent_idx, present)

def frame_index(latent_idx):
    slot_ids = jnp.arange(6, dtype=jnp.int32)
    later = 4 * latent_idx[:, None] - 5 + slot_ids[None, :]
    opening = jnp.broadcast_to(slot_ids[None, :] - 5, later.shape)
    return jnp.where(latent_idx[:, None] > 0, later, opening).astype(jnp.int32)

def norm_silu(values, gain_vec):
    mean_square = lax.optimization_barrier(jnp.mean(values * values, axis=0, keepdims=True))
    return jax.nn.silu(values * lax.rsqrt(mean_square + epsilon) * gain_vec[:, None])

def encode_group(block, opening, weights):
    w_in, b_in, g_in, w_down, b_down, g_down, w_head, b_head = weights
    channels = w_in.shape[0]
    picture = block.reshape(6, 3, PIX, PIX)
    padded = jnp.pad(picture, ((0, 0), (0, 0), (1, 1), (1, 1)))
    shifted = jnp.stack([padded[:, :, row_off:row_off + PIX, col_off:col_off + PIX] for row_off in range(3) for col_off in range(3)], axis=1)
    shifted = shifted.reshape(6, 27, PIX * PIX)
    reduced_list = []
    for frame_slot in range(4):
        columns = shifted[frame_slot:frame_slot + 3].reshape(81, PIX * PIX)
        convolved = jnp.dot(w_in, columns, preferred_element_type=jnp.float32) + b_in[:, None]
        full_res = norm_silu(convolved, g_in).astype(jnp.bfloat16)
        merged = full_res.reshape(channels, PIX // 2, 2, PIX // 2, 2).transpose(0, 2, 4, 1, 3).reshape(4 * channels, PIX // 2 * (PIX // 2))
        lowered = jnp.dot(w_down, merged, preferred_element_type=jnp.float32) + b_down[:, None]
        reduced = norm_silu(lowered, g_down).astype(jnp.bfloat16)
        if frame_slot < 3:
            reduced = jnp.where(opening, jnp.zeros_like(reduced), reduced)
        reduced_list.append(reduced)
    stacked = jnp.stack(reduced_list).reshape(4, channels, LR, 4, LR, 4).transpose(0, 1, 3, 5, 2, 4).reshape(64 * channels, LR * LR)
    latent = jnp.dot(w_head, stacked, preferred_element_type=jnp.float32) + b_head[:, None]
    return latent.reshape(-1).astype(jnp.bfloat16)

def reference(frames, latent_len, reader, owner, w_in, b_in, g_in, w_down, b_down, g_down, w_head, b_head):
    weights = (w_in, b_in, g_in, w_down, b_down, g_down, w_head, b_head)
    read_off, own_off, deal_start = clip_tables(latent_len, reader, owner)
    group_ids = jnp.arange(GROUPS, dtype=jnp.int32)
    clip_ids, latent_idx, present = find_clip(group_ids, deal_start, latent_len)
    frame_ids = frame_index(latent_idx)
    live = frame_ids >= 0
    row_ids = (reader[clip_ids] * READ_F + read_off[clip_ids]).astype(jnp.int32)[:, None] + jnp.maximum(frame_ids, 0)
    blocks = jnp.where(live[:, :, None], frames[row_ids], jnp.zeros((), frames.dtype))
    encoded = lax.map(lambda packed: encode_group(packed[0], packed[1], weights), (blocks, latent_idx == 0))
    out_rows = (owner[clip_ids] * OWN_G + own_off[clip_ids] + latent_idx).astype(jnp.int32)
    result = jnp.zeros((N_WIDE * OWN_G, encoded.shape[1]), encoded.dtype)
    return result.at[out_rows].set(encoded)
```

```python
import functools

import jax
import jax.numpy as jnp
import numpy as np
from jax import lax
from jax.experimental import pallas as pl
from jax.experimental.pallas import tpu as pltpu
from jax.sharding import PartitionSpec as P

PIX = 32
EPS = 1e-6
WIN = 48
KDIM = 160
HALF = 256
MESH = pl.DeviceIdType.MESH


def window_table():
    table = np.zeros((512, 1024), np.float32)
    for py in range(2):
        for dx in range(4):
            for u in range(8):
                for v in range(16):
                    x = 2 * v + dx - 1
                    if 0 <= x < PIX:
                        table[(2 * u + py) * PIX + x, (py * 4 + dx) * 128 + u * 16 + v] = 1
    return table


def weight_table():
    table = np.zeros((81, 1024), np.float32)
    for py in range(2):
        for px in range(2):
            for t in range(3):
                for a in range(3):
                    for b in range(3):
                        for k in range(3):
                            col = t * WIN + ((a + py) * 4 + b + px) * 3 + k
                            table[t * 27 + (a * 3 + b) * 3 + k, (py * 2 + px) * 256 + col] = 1
    return table


def down_table():
    table = np.zeros((512, 512), np.float32)
    for c in range(128):
        for ab in range(4):
            table[4 * c + ab, ab * 128 + c] = 1
    return table


def place_table():
    px = np.arange(HALF)
    place = (px // 16 // 4) * 4 + (px % 16) // 4
    return (place[:, None] == (np.arange(256) % 16)[None, :]).astype(np.float32)


def iota(shape, axis):
    return lax.broadcasted_iota(jnp.int32, shape, axis)


def column(row):
    n = row.shape[1]
    same = iota((n, n), 0) == iota((n, n), 1)
    return jnp.sum(jnp.where(same, row, jnp.zeros((), row.dtype)), axis=1, keepdims=True)


def norm_silu(values, gain):
    mean_square = jnp.sum(values * values, axis=0, keepdims=True) * (1.0 / values.shape[0])
    half = (values * gain) * (0.5 * lax.rsqrt(mean_square + EPS))
    return (half + half * jnp.tanh(half)).astype(jnp.bfloat16)


def dot(a, b):
    return jnp.dot(a, b, preferred_element_type=jnp.float32)


def encode_kernel(
    len_ref, reader_ref, frames_ref, win_ref, bin_ref, gin_ref, wdown_ref, bdown_ref, gdown_ref,
    whead_ref, bhead_ref, wtab_ref, etab_ref, dtab_ref, ptab_ref,
    out_ref, windows, w2, wd, gin_s, gdown_s, bdown_s, parts,
):
    me = lax.axis_index("wide")
    read_rows = frames_ref.shape[0]
    most = read_rows // 4
    clips = len_ref.shape[0]
    first_len = jnp.int32(0)
    seen = jnp.int32(0)
    for c in range(clips):
        mine = reader_ref[c] == me
        first_len = jnp.where(mine & (seen == 0), len_ref[c], first_len)
        seen = seen + mine.astype(jnp.int32)
    second_at = 4 * first_len - 3

    stacked = jnp.concatenate(
        [
            frames_ref[:, k * 1024 + h * 512 : k * 1024 + (h + 1) * 512]
            for k in range(3)
            for h in range(2)
        ],
        axis=0,
    )
    planes = dot(stacked, wtab_ref[...])
    lane = iota((read_rows, HALF), 1)
    for k in range(3):
        for dx in range(4):
            plane = []
            for py in range(2):
                at = (py * 4 + dx) * 128
                plane.append(
                    jnp.concatenate(
                        [
                            planes[
                                (2 * k + h) * read_rows : (2 * k + h + 1) * read_rows,
                                at : at + 128,
                            ]
                            for h in range(2)
                        ],
                        axis=1,
                    )
                )
            above = jnp.where(lane < 16, 0.0, pltpu.roll(plane[1], 16, 1))
            below = jnp.where(lane >= HALF - 16, 0.0, pltpu.roll(plane[0], HALF - 16, 1))
            for dy, value in enumerate((above, plane[0], plane[1], below)):
                row = (dy * 4 + dx) * 3 + k
                for h in range(2):
                    windows[h, pl.ds(row, read_rows, stride=WIN), :] = value[
                        :, h * 128 : (h + 1) * 128
                    ]

    spread = dot(win_ref[...], etab_ref[...])
    bias = column(bin_ref[...])
    high = bias.astype(jnp.bfloat16).astype(jnp.float32)
    mid = (bias - high).astype(jnp.bfloat16).astype(jnp.float32)
    low = bias - high - mid
    kcol = iota((128, KDIM), 1)
    tail = jnp.where(kcol == 3 * WIN, high, 0.0)
    tail = tail + jnp.where(kcol == 3 * WIN + 1, mid, 0.0)
    tail = tail + jnp.where(kcol == 3 * WIN + 2, low, 0.0)
    for ab in range(4):
        w2[ab * 128 : (ab + 1) * 128, :] = (
            spread[:, ab * 256 : ab * 256 + KDIM] + tail
        ).astype(jnp.bfloat16)
    wd[...] = dot(wdown_ref[...], dtab_ref[...]).astype(jnp.bfloat16)
    gin_s[...] = jnp.broadcast_to(column(gin_ref[...]), gin_s.shape)
    gdown_s[...] = jnp.broadcast_to(column(gdown_ref[...]), gdown_s.shape)
    bdown_s[...] = jnp.broadcast_to(column(bdown_ref[...]), bdown_s.shape)

    ones = jnp.ones((KDIM - 3 * WIN, HALF), jnp.bfloat16)

    def load(slot, count):
        at = pl.multiple_of(slot * WIN, 8)
        halves = [windows[h, pl.ds(at, count * WIN), :] for h in range(2)]
        return jnp.concatenate(halves, axis=1).astype(jnp.bfloat16)

    def encode_frame(cols):
        cols = jnp.concatenate([cols, ones], axis=0)
        full = [
            norm_silu(dot(w2[ab * 128 : (ab + 1) * 128, :], cols), gin_s[...]) for ab in range(4)
        ]
        lowered = dot(wd[...], jnp.concatenate(full, axis=0)) + bdown_s[...]
        return norm_silu(lowered, gdown_s[...])

    pix = iota((16, HALF), 1)
    sub = ((pix // 16) % 4) * 4 + pix % 4

    def keep(spot, both):
        total = jnp.zeros((16, HALF), jnp.float32)
        for ab in range(16):
            total = total + jnp.where(sub == ab, both[ab * 16 : (ab + 1) * 16, :], 0.0)
        parts[pl.ds(pl.multiple_of(spot * 16, 16), 16), :] = total

    for spot, at in enumerate((jnp.int32(0), second_at)):
        cols = load(at, 1)
        cols = jnp.concatenate([jnp.zeros((2 * WIN, HALF), jnp.bfloat16), cols], axis=0)
        keep(spot, dot(whead_ref[:, 384:512], encode_frame(cols)))

    def group(n, carry):
        second = (n >= first_len - 1).astype(jnp.int32)
        step = n + 1 - second * (first_len - 1)
        base = second * second_at + 4 * step - 5
        base = jnp.minimum(base, read_rows - 6)
        head = load(jnp.maximum(base, 0), 1)
        head = head * (step > 1).astype(jnp.bfloat16)
        cols = jnp.concatenate([head, load(base + 1, 5)], axis=0)
        reduced = jnp.concatenate(
            [encode_frame(cols[s * WIN : (s + 3) * WIN, :]) for s in range(4)], axis=0
        )
        keep(n + 2, dot(whead_ref[...], reduced))
        return carry

    lax.fori_loop(0, most - 2, group, 0)

    rows = most * 16
    value = parts[...]
    top = value.astype(jnp.bfloat16)
    rest = (value - top.astype(jnp.float32)).astype(jnp.bfloat16)
    wide = dot(top, ptab_ref[...]) + dot(rest, ptab_ref[...])
    match = iota((rows, 256), 1) // 16 == iota((rows, 256), 0) % 16
    wide = jnp.where(match, wide, 0.0).reshape(most, 16, 256)
    bh = jnp.where(
        iota((16, 256), 1) // 16 == iota((16, 256), 0), column(bhead_ref[...]), 0.0
    )
    bh = jnp.sum(bh, axis=0, keepdims=True)
    result = jnp.sum(wide, axis=1) + bh
    out_rows = out_ref.shape[0]
    if out_rows > most:
        result = jnp.concatenate([result, jnp.zeros((out_rows - most, 256), jnp.float32)], axis=0)
    out_ref[...] = result.astype(jnp.bfloat16)


def spread_kernel(enc_ref, len_ref, reader_ref, owner_ref, out_ref, held, send_sem, recv_sem):
    me = lax.axis_index("wide")
    n, rows = held.shape[0], held.shape[1]
    barrier = pltpu.get_barrier_semaphore()
    for d in range(1, n):
        pl.semaphore_signal(
            barrier, inc=1, device_id={"wide": lax.rem(me + d, n)}, device_id_type=MESH
        )
    pl.semaphore_wait(barrier, n - 1)
    copies = []
    for d in range(1, n):
        copy = pltpu.make_async_remote_copy(
            src_ref=enc_ref,
            dst_ref=held.at[me],
            send_sem=send_sem.at[d],
            recv_sem=recv_sem.at[d],
            device_id={"wide": lax.rem(me + d, n)},
            device_id_type=MESH,
        )
        copy.start()
        copies.append(copy)
    held[me] = enc_ref[...]

    own_rows = out_ref.shape[0]
    clips = len_ref.shape[1]
    len_row, reader_row, owner_row = (
        ref[...].astype(jnp.float32) for ref in (len_ref, reader_ref, owner_ref)
    )
    len_col, reader_col, owner_col = column(len_row), column(reader_row), column(owner_row)
    earlier = iota((clips, clips), 1) < iota((clips, clips), 0)
    before_here = jnp.sum(
        jnp.where(earlier & (reader_row == reader_col), len_row, 0.0), axis=1, keepdims=True
    )
    own_off = jnp.sum(
        jnp.where(earlier & (owner_row == owner_col), len_row, 0.0), axis=1, keepdims=True
    )
    slot = iota((clips, 128), 1).astype(jnp.float32)
    step = slot - own_off
    inside = (owner_col == me.astype(jnp.float32)) & (step >= 0.0) & (step < len_col)
    late = before_here > 0.0
    opening = jnp.where(late, 1.0, 0.0)
    later = jnp.where(late, before_here, 1.0) + step
    source = reader_col * rows + jnp.where(step == 0.0, opening, later)
    picked = jnp.sum(jnp.where(inside, source + 1.0, 0.0), axis=0, keepdims=True) - 1.0
    pick = (iota((n * rows, 128), 0).astype(jnp.float32) == picked).astype(jnp.float32)
    pick = pick.T.astype(jnp.bfloat16)

    for copy in copies:
        copy.wait()
    result = dot(pick, held[...].reshape(n * rows, 256))
    out_ref[...] = result[:own_rows].astype(jnp.bfloat16)


def shards(
    frames, latent_len, reader, owner, w_in, b_in, g_in, w_down, b_down, g_down, w_head, b_head
):
    n = lax.axis_size("wide")
    read_rows = frames.shape[0]
    most = read_rows // 4
    held_rows = -(-most // 16) * 16
    own_rows = 2 * ((most + 2) // 2)
    heads = w_head.reshape(16, 512, 16).transpose(2, 0, 1).reshape(256, 512)
    vmem = pl.BlockSpec(memory_space=pltpu.VMEM)
    smem = pl.BlockSpec(memory_space=pltpu.SMEM)
    tables = [
        jnp.asarray(t, dtype=jnp.bfloat16)
        for t in (window_table(), weight_table(), down_table(), place_table())
    ]
    encoded = pl.pallas_call(
        encode_kernel,
        out_shape=jax.ShapeDtypeStruct((held_rows, 256), jnp.bfloat16),
        in_specs=[smem] * 2 + [vmem] * 13,
        out_specs=vmem,
        scratch_shapes=[
            pltpu.VMEM((2, read_rows * WIN, 128), jnp.float32),
            pltpu.VMEM((512, KDIM), jnp.bfloat16),
            pltpu.VMEM((128, 512), jnp.bfloat16),
            pltpu.VMEM((128, HALF), jnp.float32),
            pltpu.VMEM((128, HALF), jnp.float32),
            pltpu.VMEM((128, HALF), jnp.float32),
            pltpu.VMEM((most * 16, HALF), jnp.float32),
        ],
        compiler_params=pltpu.CompilerParams(vmem_limit_bytes=48 * 1024 * 1024),
        name="encode",
    )(
        latent_len, reader, frames, w_in, b_in[None, :], g_in[None, :], w_down, b_down[None, :],
        g_down[None, :], heads, b_head[None, :], *tables,
    )
    return pl.pallas_call(
        spread_kernel,
        out_shape=jax.ShapeDtypeStruct((own_rows, 256), jnp.bfloat16),
        in_specs=[vmem] * 4,
        out_specs=vmem,
        scratch_shapes=[
            pltpu.VMEM((n, held_rows, 256), jnp.bfloat16),
            pltpu.SemaphoreType.DMA((n,)),
            pltpu.SemaphoreType.DMA((n,)),
        ],
        compiler_params=pltpu.CompilerParams(
            collective_id=0, has_side_effects=True, vmem_limit_bytes=32 * 1024 * 1024
        ),
        name="spread",
    )(encoded, latent_len[None, :], reader[None, :], owner[None, :])


def solution(mesh):
    return jax.shard_map(
        shards,
        mesh=mesh,
        in_specs=(
            P(("groups", "wide"), None),
            P("groups"),
            P("groups"),
            P("groups"),
            P(),
            P(),
            P(),
            P(),
            P(),
            P(),
            P(),
            P(),
        ),
        out_specs=P(("groups", "wide"), None),
        check_vma=False,
    )
```

```python
import functools

import jax
import jax.numpy as jnp
import numpy as np
from jax import lax
from jax.experimental import pallas as pl
from jax.experimental.pallas import tpu as pltpu
from jax.sharding import PartitionSpec as P

PIX = 32
EPS = 1e-6
WIN = 48
KDIM = 160
HALF = 256
MESH = pl.DeviceIdType.MESH


def window_table():
    table = np.zeros((512, 1024), np.float32)
    for py in range(2):
        for dx in range(4):
            for u in range(8):
                for v in range(16):
                    x = 2 * v + dx - 1
                    if 0 <= x < PIX:
                        table[(2 * u + py) * PIX + x, (py * 4 + dx) * 128 + u * 16 + v] = 1
    return table


def weight_table():
    table = np.zeros((81, 1024), np.float32)
    for py in range(2):
        for px in range(2):
            for t in range(3):
                for a in range(3):
                    for b in range(3):
                        for k in range(3):
                            col = t * WIN + ((a + py) * 4 + b + px) * 3 + k
                            table[t * 27 + (a * 3 + b) * 3 + k, (py * 2 + px) * 256 + col] = 1
    return table


def down_table():
    table = np.zeros((512, 512), np.float32)
    for c in range(128):
        for ab in range(4):
            table[4 * c + ab, ab * 128 + c] = 1
    return table


def place_table():
    px = np.arange(HALF)
    place = (px // 16 // 4) * 4 + (px % 16) // 4
    return (place[:, None] == (np.arange(256) % 16)[None, :]).astype(np.float32)


def head_table():
    table = np.zeros((256, 256), np.float32)
    for j in range(16):
        for ab in range(16):
            table[j * 16 + ab, ab * 16 + j] = 1
    return table


def iota(shape, axis):
    return lax.broadcasted_iota(jnp.int32, shape, axis)


def column(row):
    n = row.shape[1]
    same = iota((n, n), 0) == iota((n, n), 1)
    return jnp.sum(jnp.where(same, row, jnp.zeros((), row.dtype)), axis=1, keepdims=True)


def norm_silu(values, gain):
    mean_square = jnp.sum(values * values, axis=0, keepdims=True) * (1.0 / values.shape[0])
    half = (values * gain) * (0.5 * lax.rsqrt(mean_square + EPS))
    return (half + half * jnp.tanh(half)).astype(jnp.bfloat16)


def norm_silu_packed(values, gain):
    count = values.shape[0]
    packed = values.astype(jnp.bfloat16)
    squares = packed * packed
    while squares.shape[0] > 16:
        middle = squares.shape[0] // 2
        squares = squares[:middle] + squares[middle:]
    mean_square = jnp.sum(squares.astype(jnp.float32), axis=0, keepdims=True) * (1.0 / count)
    scale = (0.5 * lax.rsqrt(mean_square + EPS)).astype(jnp.bfloat16)
    half = (packed * gain) * scale
    return half + half * jnp.tanh(half)


def dot(a, b):
    return jnp.dot(a, b, preferred_element_type=jnp.float32)


def kernel(
    lens_ref, readers_ref, owners_ref, frames_ref, win_ref, bin_ref, gin_ref,
    wdown_ref, bdown_ref, gdown_ref, whead_ref, bhead_ref, wtab_ref, etab_ref, dtab_ref, htab_ref,
    ptab_ref, out_ref, windows, w2, wd, heads, gin_s, gdown_s, bdown_s, parts, flags, enc, held, pick_s,
    send_sem, recv_sem,
):
    me = lax.axis_index("wide")
    n, rows = held.shape[0], held.shape[1]
    barrier = pltpu.get_barrier_semaphore()
    for d in range(1, n):
        pl.semaphore_signal(
            barrier, inc=1, device_id={"wide": lax.rem(me + d, n)}, device_id_type=MESH
        )
    read_rows = frames_ref.shape[0]
    most = read_rows // 4
    clips = lens_ref.shape[1]
    mine_at = me.astype(jnp.float32)
    len_row, reader_row, owner_row = (
        ref[...].astype(jnp.float32) for ref in (lens_ref, readers_ref, owners_ref)
    )
    len_col, reader_col, owner_col = column(len_row), column(reader_row), column(owner_row)
    earlier = iota((clips, clips), 1) < iota((clips, clips), 0)
    before_here = jnp.sum(
        jnp.where(earlier & (reader_row == reader_col), len_row, 0.0), axis=1, keepdims=True
    )
    first_len = jnp.sum(
        jnp.where((reader_col == mine_at) & (before_here == 0.0), len_col, 0.0),
        axis=0,
        keepdims=True,
    )

    last = 4 * most - 6
    row = iota((read_rows, 1), 0)
    number = ((row + 2) // 4 - 1).astype(jnp.float32)
    offset = ((row + 2) % 4).astype(jnp.float32)
    second = jnp.where(number >= first_len - 1.0, 1.0, 0.0)
    step = number + 1.0 - second * (first_len - 1.0)
    second_at = 4.0 * first_len - 3.0
    source = second * second_at + 4.0 * step - 3.0 + offset
    source = jnp.where(row < last, source, -1.0)
    source = jnp.where(row == 0, -1.0, source)
    source = jnp.where(row == 1, 0.0, source)
    source = jnp.where(row == last + 1, second_at, source)
    order = (iota((read_rows, read_rows), 1).astype(jnp.float32) == source).astype(jnp.bfloat16)
    frames = dot(order, frames_ref[...]).astype(jnp.bfloat16)
    flags[...] = jnp.where(
        iota(flags.shape, 0).astype(jnp.float32) == first_len - 1.0, 1.0, 0.0
    ) * jnp.ones(flags.shape, jnp.float32)

    stacked = jnp.concatenate(
        [
            frames[:, k * 1024 + h * 512 : k * 1024 + (h + 1) * 512]
            for k in range(3)
            for h in range(2)
        ],
        axis=0,
    )
    planes = dot(stacked, wtab_ref[...])
    lane = iota((read_rows, HALF), 1)
    for k in range(3):
        for dx in range(4):
            plane = []
            for py in range(2):
                at = (py * 4 + dx) * 128
                plane.append(
                    jnp.concatenate(
                        [
                            planes[
                                (2 * k + h) * read_rows : (2 * k + h + 1) * read_rows,
                                at : at + 128,
                            ]
                            for h in range(2)
                        ],
                        axis=1,
                    )
                )
            above = jnp.where(lane < 16, 0.0, pltpu.roll(plane[1], 16, 1))
            below = jnp.where(lane >= HALF - 16, 0.0, pltpu.roll(plane[0], HALF - 16, 1))
            for dy, value in enumerate((above, plane[0], plane[1], below)):
                row = (dy * 4 + dx) * 3 + k
                for h in range(2):
                    windows[h, pl.ds(row, read_rows, stride=WIN), :] = value[
                        :, h * 128 : (h + 1) * 128
                    ]

    spread = dot(win_ref[...], etab_ref[...])
    bias = column(bin_ref[...])
    high = bias.astype(jnp.bfloat16).astype(jnp.float32)
    mid = (bias - high).astype(jnp.bfloat16).astype(jnp.float32)
    low = bias - high - mid
    kcol = iota((128, KDIM), 1)
    tail = jnp.where(kcol == 3 * WIN, high, 0.0)
    tail = tail + jnp.where(kcol == 3 * WIN + 1, mid, 0.0)
    tail = tail + jnp.where(kcol == 3 * WIN + 2, low, 0.0)
    for ab in range(4):
        w2[ab * 128 : (ab + 1) * 128, :] = (
            spread[:, ab * 256 : ab * 256 + KDIM] + tail
        ).astype(jnp.bfloat16)
    wd[...] = dot(wdown_ref[...], dtab_ref[...]).astype(jnp.bfloat16)
    gin_s[...] = jnp.broadcast_to(column(gin_ref[...]), gin_s.shape).astype(jnp.bfloat16)
    gdown_s[...] = jnp.broadcast_to(column(gdown_ref[...]), gdown_s.shape)
    bdown_s[...] = jnp.broadcast_to(column(bdown_ref[...]), bdown_s.shape)

    chunks = jnp.concatenate(
        [whead_ref[:, (s * 8 + c) * 256 : (s * 8 + c + 1) * 256] for c in range(8) for s in range(4)],
        axis=0,
    )
    turned = dot(chunks, htab_ref[...])
    piece = iota((64, 128), 1) // 16
    for ab in range(16):
        at = ab // 8 * 128
        row = jnp.zeros((64, 128), jnp.float32)
        for c in range(8):
            value = turned[c * 64 : (c + 1) * 64, at : at + 128]
            shift = (16 * c - ab % 8 * 16) % 128
            value = pltpu.roll(value, shift, 1) if shift else value
            row = jnp.where(piece == c, value, row)
        row = row.astype(jnp.bfloat16)
        for s in range(4):
            heads[ab * 16 : (ab + 1) * 16, s * 128 : (s + 1) * 128] = row[s * 16 : (s + 1) * 16]

    own_rows = out_ref.shape[0]
    own_off = jnp.sum(
        jnp.where(earlier & (owner_row == owner_col), len_row, 0.0), axis=1, keepdims=True
    )
    slot = iota((clips, 128), 1).astype(jnp.float32)
    place = slot - own_off
    inside = (owner_col == mine_at) & (place >= 0.0) & (place < len_col)
    late = before_here > 0.0
    opening = jnp.where(late, 1.0, 0.0)
    later = jnp.where(late, before_here, 1.0) + place
    source = reader_col * rows + jnp.where(place == 0.0, opening, later)
    picked = jnp.sum(jnp.where(inside, source + 1.0, 0.0), axis=0, keepdims=True) - 1.0
    pick = (iota((n * rows, 128), 0).astype(jnp.float32) == picked).astype(jnp.float32)
    pick_s[...] = pick.T.astype(jnp.bfloat16)

    ones = jnp.ones((KDIM - 3 * WIN, HALF), jnp.bfloat16)

    def load(slot, count):
        at = pl.multiple_of(slot * WIN, 8)
        halves = [windows[h, pl.ds(at, count * WIN), :] for h in range(2)]
        return jnp.concatenate(halves, axis=1)

    def encode_frame(cols):
        cols = jnp.concatenate([cols, ones], axis=0)
        full = [
            norm_silu_packed(dot(w2[ab * 128 : (ab + 1) * 128, :], cols), gin_s[...]) for ab in range(4)
        ]
        lowered = dot(wd[...], jnp.concatenate(full, axis=0)) + bdown_s[...]
        return norm_silu(lowered, gdown_s[...])

    pix = iota((16, HALF), 1)
    sub = ((pix // 16) % 4) * 4 + pix % 4

    def keep(spot, both):
        total = jnp.zeros((16, HALF), jnp.float32)
        for ab in range(16):
            total = total + jnp.where(sub == ab, both[ab * 16 : (ab + 1) * 16, :], 0.0)
        parts[pl.ds(pl.multiple_of(spot * 16, 16), 16), :] = total

    for spot, at in enumerate((1, last + 1)):
        cols = load(at, 1).astype(jnp.bfloat16)
        cols = jnp.concatenate([jnp.zeros((2 * WIN, HALF), jnp.bfloat16), cols], axis=0)
        keep(spot, dot(heads[:, 384:512], encode_frame(cols)))

    def group(at, carry):
        flag = flags[pl.ds(at, 1), :]
        before = load(4 * at, 2) * (1.0 - flag) + load(last, 2) * flag
        cols = jnp.concatenate([before, load(4 * at + 2, 4)], axis=0).astype(jnp.bfloat16)
        reduced = jnp.concatenate(
            [encode_frame(cols[s * WIN : (s + 3) * WIN, :]) for s in range(4)], axis=0
        )
        keep(at + 2, dot(heads[...], reduced))
        return carry

    lax.fori_loop(0, most - 2, group, 0)

    value = parts[...]
    top = value.astype(jnp.bfloat16)
    rest = (value - top.astype(jnp.float32)).astype(jnp.bfloat16)
    wide = dot(top, ptab_ref[...]) + dot(rest, ptab_ref[...])
    match = iota((most * 16, 256), 1) // 16 == iota((most * 16, 256), 0) % 16
    wide = jnp.where(match, wide, 0.0).reshape(most, 16, 256)
    bh = jnp.where(
        iota((16, 256), 1) // 16 == iota((16, 256), 0), column(bhead_ref[...]), 0.0
    )
    bh = jnp.sum(bh, axis=0, keepdims=True)
    result = jnp.sum(wide, axis=1) + bh
    if rows > most:
        result = jnp.concatenate([result, jnp.zeros((rows - most, 256), jnp.float32)], axis=0)
    enc[...] = result.astype(jnp.bfloat16)

    pl.semaphore_wait(barrier, n - 1)
    copies = []
    for d in range(1, n):
        copy = pltpu.make_async_remote_copy(
            src_ref=enc,
            dst_ref=held.at[me],
            send_sem=send_sem.at[d],
            recv_sem=recv_sem.at[d],
            device_id={"wide": lax.rem(me + d, n)},
            device_id_type=MESH,
        )
        copy.start()
        copies.append(copy)
    held[me] = enc[...]
    for copy in copies:
        copy.wait()
    result = dot(pick_s[...], held[...].reshape(n * rows, 256))
    out_ref[...] = result[:own_rows].astype(jnp.bfloat16)


def shards(
    frames, latent_len, reader, owner, w_in, b_in, g_in, w_down, b_down, g_down, w_head, b_head
):
    n = lax.axis_size("wide")
    read_rows = frames.shape[0]
    most = read_rows // 4
    held_rows = -(-most // 16) * 16
    own_rows = 2 * ((most + 2) // 2)
    vmem = pl.BlockSpec(memory_space=pltpu.VMEM)
    tables = [
        jnp.asarray(t, dtype=jnp.bfloat16)
        for t in (window_table(), weight_table(), down_table(), head_table(), place_table())
    ]
    return pl.pallas_call(
        kernel,
        out_shape=jax.ShapeDtypeStruct((own_rows, 256), jnp.bfloat16),
        in_specs=[vmem] * 17,
        out_specs=vmem,
        scratch_shapes=[
            pltpu.VMEM((2, read_rows * WIN, 128), jnp.float32),
            pltpu.VMEM((512, KDIM), jnp.bfloat16),
            pltpu.VMEM((128, 512), jnp.bfloat16),
            pltpu.VMEM((256, 512), jnp.bfloat16),
            pltpu.VMEM((128, HALF), jnp.bfloat16),
            pltpu.VMEM((128, HALF), jnp.float32),
            pltpu.VMEM((128, HALF), jnp.float32),
            pltpu.VMEM((most * 16, HALF), jnp.float32),
            pltpu.VMEM((most, HALF), jnp.float32),
            pltpu.VMEM((held_rows, 256), jnp.bfloat16),
            pltpu.VMEM((n, held_rows, 256), jnp.bfloat16),
            pltpu.VMEM((128, n * held_rows), jnp.bfloat16),
            pltpu.SemaphoreType.DMA((n,)),
            pltpu.SemaphoreType.DMA((n,)),
        ],
        compiler_params=pltpu.CompilerParams(
            collective_id=0, has_side_effects=True, vmem_limit_bytes=48 * 1024 * 1024
        ),
        name="encode",
    )(
        latent_len[None, :], reader[None, :], owner[None, :], frames, w_in,
        b_in[None, :], g_in[None, :], w_down, b_down[None, :], g_down[None, :], w_head,
        b_head[None, :], *tables,
    )


def solution(mesh):
    return jax.shard_map(
        shards,
        mesh=mesh,
        in_specs=(
            P(("groups", "wide"), None),
            P("groups"),
            P("groups"),
            P("groups"),
            P(),
            P(),
            P(),
            P(),
            P(),
            P(),
            P(),
            P(),
        ),
        out_specs=P(("groups", "wide"), None),
        check_vma=False,
    )
```

```python
import functools

import jax
import jax.numpy as jnp
import numpy as np
from jax import lax
from jax.experimental import pallas as pl
from jax.experimental.pallas import tpu as pltpu
from jax.sharding import PartitionSpec as P

PIX = 32
EPS = 1e-6
WIN = 48
KDIM = 160
HALF = 256
MESH = pl.DeviceIdType.MESH


def window_table():
    table = np.zeros((512, 1024), np.float32)
    for py in range(2):
        for dx in range(4):
            for u in range(8):
                for v in range(16):
                    x = 2 * v + dx - 1
                    if 0 <= x < PIX:
                        table[(2 * u + py) * PIX + x, (py * 4 + dx) * 128 + u * 16 + v] = 1
    return table


def weight_table():
    table = np.zeros((81, 1024), np.float32)
    for py in range(2):
        for px in range(2):
            for t in range(3):
                for a in range(3):
                    for b in range(3):
                        for k in range(3):
                            col = t * WIN + ((a + py) * 4 + b + px) * 3 + k
                            table[t * 27 + (a * 3 + b) * 3 + k, (py * 2 + px) * 256 + col] = 1
    return table


def down_table():
    table = np.zeros((512, 512), np.float32)
    for c in range(128):
        for ab in range(4):
            table[4 * c + ab, ab * 128 + c] = 1
    return table


def place_table():
    px = np.arange(HALF)
    place = (px // 16 // 4) * 4 + (px % 16) // 4
    return (place[:, None] == (np.arange(256) % 16)[None, :]).astype(np.float32)


def head_table():
    table = np.zeros((256, 256), np.float32)
    for j in range(16):
        for ab in range(16):
            table[j * 16 + ab, ab * 16 + j] = 1
    return table


def iota(shape, axis):
    return lax.broadcasted_iota(jnp.int32, shape, axis)


def column(row):
    n = row.shape[1]
    same = iota((n, n), 0) == iota((n, n), 1)
    return jnp.sum(jnp.where(same, row, jnp.zeros((), row.dtype)), axis=1, keepdims=True)


def norm_silu(values, gain):
    mean_square = jnp.sum(values * values, axis=0, keepdims=True) * (1.0 / values.shape[0])
    half = (values * gain) * (0.5 * lax.rsqrt(mean_square + EPS))
    return (half + half * jnp.tanh(half)).astype(jnp.bfloat16)


def dot(a, b):
    return jnp.dot(a, b, preferred_element_type=jnp.float32)


def kernel(*refs):
    sources, (out_ref, *rest) = refs[:17], refs[17:]
    loaded, rest = rest[:17], rest[17:]
    (windows, w2, wd, heads, gin_s, gdown_s, bdown_s, parts, flags, enc, held, pick_s) = rest[:12]
    load_sem, send_sem, recv_sem = rest[12:]
    loads = [
        pltpu.make_async_copy(source, target, load_sem.at[at])
        for at, (source, target) in enumerate(zip(sources, loaded))
    ]
    for load in loads:
        load.start()
    (
        lens_ref, readers_ref, owners_ref, frames_ref, wtab_ref, win_ref, bin_ref, gin_ref,
        wdown_ref, bdown_ref, gdown_ref, whead_ref, bhead_ref, etab_ref, dtab_ref, htab_ref,
        ptab_ref,
    ) = loaded
    me = lax.axis_index("wide")
    n, rows = held.shape[0], held.shape[1]
    barrier = pltpu.get_barrier_semaphore()
    for d in range(1, n):
        pl.semaphore_signal(
            barrier, inc=1, device_id={"wide": lax.rem(me + d, n)}, device_id_type=MESH
        )
    for load in loads:
        load.wait()
    read_rows = frames_ref.shape[0]
    most = read_rows // 4
    clips = lens_ref.shape[1]
    mine_at = me.astype(jnp.float32)
    len_row, reader_row, owner_row = (
        ref[...].astype(jnp.float32) for ref in (lens_ref, readers_ref, owners_ref)
    )
    len_col, reader_col, owner_col = column(len_row), column(reader_row), column(owner_row)
    earlier = iota((clips, clips), 1) < iota((clips, clips), 0)
    before_here = jnp.sum(
        jnp.where(earlier & (reader_row == reader_col), len_row, 0.0), axis=1, keepdims=True
    )
    first_len = jnp.sum(
        jnp.where((reader_col == mine_at) & (before_here == 0.0), len_col, 0.0),
        axis=0,
        keepdims=True,
    )

    last = 4 * most - 6
    row = iota((read_rows, 1), 0)
    number = ((row + 2) // 4 - 1).astype(jnp.float32)
    offset = ((row + 2) % 4).astype(jnp.float32)
    second = jnp.where(number >= first_len - 1.0, 1.0, 0.0)
    step = number + 1.0 - second * (first_len - 1.0)
    second_at = 4.0 * first_len - 3.0
    source = second * second_at + 4.0 * step - 3.0 + offset
    source = jnp.where(row < last, source, -1.0)
    source = jnp.where(row == 0, -1.0, source)
    source = jnp.where(row == 1, 0.0, source)
    source = jnp.where(row == last + 1, second_at, source)
    order = (iota((read_rows, read_rows), 1).astype(jnp.float32) == source).astype(jnp.bfloat16)
    frames = dot(order, frames_ref[...]).astype(jnp.bfloat16)
    flags[...] = jnp.where(
        iota(flags.shape, 0).astype(jnp.float32) == first_len - 1.0, 1.0, 0.0
    ) * jnp.ones(flags.shape, jnp.float32)

    stacked = jnp.concatenate(
        [
            frames[:, k * 1024 + h * 512 : k * 1024 + (h + 1) * 512]
            for k in range(3)
            for h in range(2)
        ],
        axis=0,
    )
    planes = dot(stacked, wtab_ref[...])
    lane = iota((read_rows, HALF), 1)
    for k in range(3):
        for dx in range(4):
            plane = []
            for py in range(2):
                at = (py * 4 + dx) * 128
                plane.append(
                    jnp.concatenate(
                        [
                            planes[
                                (2 * k + h) * read_rows : (2 * k + h + 1) * read_rows,
                                at : at + 128,
                            ]
                            for h in range(2)
                        ],
                        axis=1,
                    )
                )
            above = jnp.where(lane < 16, 0.0, pltpu.roll(plane[1], 16, 1))
            below = jnp.where(lane >= HALF - 16, 0.0, pltpu.roll(plane[0], HALF - 16, 1))
            for dy, value in enumerate((above, plane[0], plane[1], below)):
                row = (dy * 4 + dx) * 3 + k
                for h in range(2):
                    windows[h, pl.ds(row, read_rows, stride=WIN), :] = value[
                        :, h * 128 : (h + 1) * 128
                    ]

    spread = lax.dot_general(
        win_ref[...], etab_ref[...], (((0,), (0,)), ((), ())), preferred_element_type=jnp.float32
    )
    bias = column(bin_ref[...])
    high = bias.astype(jnp.bfloat16).astype(jnp.float32)
    mid = (bias - high).astype(jnp.bfloat16).astype(jnp.float32)
    low = bias - high - mid
    kcol = iota((128, KDIM), 1)
    tail = jnp.where(kcol == 3 * WIN, high, 0.0)
    tail = tail + jnp.where(kcol == 3 * WIN + 1, mid, 0.0)
    tail = tail + jnp.where(kcol == 3 * WIN + 2, low, 0.0)
    for ab in range(4):
        w2[ab * 128 : (ab + 1) * 128, :] = (
            spread[:, ab * 256 : ab * 256 + KDIM] + tail
        ).astype(jnp.bfloat16)
    wd[...] = dot(wdown_ref[...], dtab_ref[...]).astype(jnp.bfloat16)
    gin_s[...] = jnp.broadcast_to(column(gin_ref[...]), gin_s.shape)
    gdown_s[...] = jnp.broadcast_to(column(gdown_ref[...]), gdown_s.shape)
    bdown_s[...] = jnp.broadcast_to(column(bdown_ref[...]), bdown_s.shape)

    chunks = jnp.concatenate(
        [whead_ref[:, (s * 8 + c) * 256 : (s * 8 + c + 1) * 256] for c in range(8) for s in range(4)],
        axis=0,
    )
    turned = dot(chunks, htab_ref[...])
    piece = iota((64, 128), 1) // 16
    for ab in range(16):
        at = ab // 8 * 128
        row = jnp.zeros((64, 128), jnp.float32)
        for c in range(8):
            value = turned[c * 64 : (c + 1) * 64, at : at + 128]
            shift = (16 * c - ab % 8 * 16) % 128
            value = pltpu.roll(value, shift, 1) if shift else value
            row = jnp.where(piece == c, value, row)
        row = row.astype(jnp.bfloat16)
        for s in range(4):
            heads[ab * 16 : (ab + 1) * 16, s * 128 : (s + 1) * 128] = row[s * 16 : (s + 1) * 16]

    own_rows = out_ref.shape[0]
    own_off = jnp.sum(
        jnp.where(earlier & (owner_row == owner_col), len_row, 0.0), axis=1, keepdims=True
    )
    slot = iota((clips, 128), 1).astype(jnp.float32)
    place = slot - own_off
    inside = (owner_col == mine_at) & (place >= 0.0) & (place < len_col)
    late = before_here > 0.0
    opening = jnp.where(late, 1.0, 0.0)
    later = jnp.where(late, before_here, 1.0) + place
    source = reader_col * rows + jnp.where(place == 0.0, opening, later)
    picked = jnp.sum(jnp.where(inside, source + 1.0, 0.0), axis=0, keepdims=True) - 1.0
    pick = (iota((n * rows, 128), 0).astype(jnp.float32) == picked).astype(jnp.float32)
    pick_s[...] = pick.T.astype(jnp.bfloat16)

    ones = jnp.ones((KDIM - 3 * WIN, HALF), jnp.bfloat16)

    def window(slot, count):
        at = pl.multiple_of(slot * WIN, 8)
        halves = [windows[h, pl.ds(at, count * WIN), :] for h in range(2)]
        return jnp.concatenate(halves, axis=1)

    def encode_frame(cols):
        cols = jnp.concatenate([cols, ones], axis=0)
        convolved = dot(w2[...], cols)
        full = [
            norm_silu(convolved[ab * 128 : (ab + 1) * 128, :], gin_s[...]) for ab in range(4)
        ]
        lowered = dot(wd[...], jnp.concatenate(full, axis=0)) + bdown_s[...]
        return norm_silu(lowered, gdown_s[...])

    pix = iota((16, HALF), 1)
    sub = ((pix // 16) % 4) * 4 + pix % 4

    def keep(spot, both):
        total = jnp.zeros((16, HALF), jnp.float32)
        for ab in range(16):
            total = total + jnp.where(sub == ab, both[ab * 16 : (ab + 1) * 16, :], 0.0)
        parts[pl.ds(pl.multiple_of(spot * 16, 16), 16), :] = total

    for spot, at in enumerate((1, last + 1)):
        cols = window(at, 1).astype(jnp.bfloat16)
        cols = jnp.concatenate([jnp.zeros((2 * WIN, HALF), jnp.bfloat16), cols], axis=0)
        keep(spot, dot(heads[:, 384:512], encode_frame(cols)))

    def group(at, carry):
        flag = flags[pl.ds(at, 1), :]
        before = window(4 * at, 2) * (1.0 - flag) + window(last, 2) * flag
        cols = jnp.concatenate([before, window(4 * at + 2, 4)], axis=0).astype(jnp.bfloat16)
        reduced = jnp.concatenate(
            [encode_frame(cols[s * WIN : (s + 3) * WIN, :]) for s in range(4)], axis=0
        )
        keep(at + 2, dot(heads[...], reduced))
        return carry

    lax.fori_loop(0, most - 2, group, 0)

    value = parts[...]
    top = value.astype(jnp.bfloat16)
    rest = (value - top.astype(jnp.float32)).astype(jnp.bfloat16)
    wide = dot(top, ptab_ref[...]) + dot(rest, ptab_ref[...])
    match = iota((most * 16, 256), 1) // 16 == iota((most * 16, 256), 0) % 16
    wide = jnp.where(match, wide, 0.0).reshape(most, 16, 256)
    bh = jnp.where(
        iota((16, 256), 1) // 16 == iota((16, 256), 0), column(bhead_ref[...]), 0.0
    )
    bh = jnp.sum(bh, axis=0, keepdims=True)
    result = jnp.sum(wide, axis=1) + bh
    if rows > most:
        result = jnp.concatenate([result, jnp.zeros((rows - most, 256), jnp.float32)], axis=0)
    enc[...] = result.astype(jnp.bfloat16)

    pl.semaphore_wait(barrier, n - 1)
    copies = []
    for d in range(1, n):
        copy = pltpu.make_async_remote_copy(
            src_ref=enc,
            dst_ref=held.at[me],
            send_sem=send_sem.at[d],
            recv_sem=recv_sem.at[d],
            device_id={"wide": lax.rem(me + d, n)},
            device_id_type=MESH,
        )
        copy.start()
        copies.append(copy)
    held[me] = enc[...]
    for copy in copies:
        copy.wait()
    result = dot(pick_s[...], held[...].reshape(n * rows, 256))
    out_ref[...] = result[:own_rows].astype(jnp.bfloat16)


def shards(
    frames, latent_len, reader, owner, w_in, b_in, g_in, w_down, b_down, g_down, w_head, b_head
):
    n = lax.axis_size("wide")
    read_rows = frames.shape[0]
    most = read_rows // 4
    held_rows = -(-most // 16) * 16
    own_rows = 2 * ((most + 2) // 2)
    hbm = pl.BlockSpec(memory_space=pltpu.HBM)
    vmem = pl.BlockSpec(memory_space=pltpu.VMEM)
    wtab, etab, dtab, htab, ptab = (
        jnp.asarray(t, dtype=jnp.bfloat16)
        for t in (window_table(), weight_table(), down_table(), head_table(), place_table())
    )
    operands = (
        latent_len[None, :], reader[None, :], owner[None, :], frames, wtab, w_in.T,
        b_in[None, :], g_in[None, :], w_down, b_down[None, :], g_down[None, :], w_head,
        b_head[None, :], etab, dtab, htab, ptab,
    )
    return pl.pallas_call(
        kernel,
        out_shape=jax.ShapeDtypeStruct((own_rows, 256), jnp.bfloat16),
        in_specs=[hbm] * len(operands),
        out_specs=vmem,
        scratch_shapes=[pltpu.VMEM(value.shape, value.dtype) for value in operands]
        + [
            pltpu.VMEM((2, read_rows * WIN, 128), jnp.float32),
            pltpu.VMEM((512, KDIM), jnp.bfloat16),
            pltpu.VMEM((128, 512), jnp.bfloat16),
            pltpu.VMEM((256, 512), jnp.bfloat16),
            pltpu.VMEM((128, HALF), jnp.float32),
            pltpu.VMEM((128, HALF), jnp.float32),
            pltpu.VMEM((128, HALF), jnp.float32),
            pltpu.VMEM((most * 16, HALF), jnp.float32),
            pltpu.VMEM((most, HALF), jnp.float32),
            pltpu.VMEM((held_rows, 256), jnp.bfloat16),
            pltpu.VMEM((n, held_rows, 256), jnp.bfloat16),
            pltpu.VMEM((128, n * held_rows), jnp.bfloat16),
            pltpu.SemaphoreType.DMA((len(operands),)),
            pltpu.SemaphoreType.DMA((n,)),
            pltpu.SemaphoreType.DMA((n,)),
        ],
        compiler_params=pltpu.CompilerParams(
            collective_id=0, has_side_effects=True, vmem_limit_bytes=56 * 1024 * 1024
        ),
        name="encode",
    )(*operands)


def solution(mesh):
    return jax.shard_map(
        shards,
        mesh=mesh,
        in_specs=(
            P(("groups", "wide"), None),
            P("groups"),
            P("groups"),
            P("groups"),
            P(),
            P(),
            P(),
            P(),
            P(),
            P(),
            P(),
            P(),
        ),
        out_specs=P(("groups", "wide"), None),
        check_vma=False,
    )
```

```python
import functools

import jax
import jax.numpy as jnp
import numpy as np
from jax import lax
from jax.experimental import pallas as pl
from jax.experimental.pallas import tpu as pltpu
from jax.sharding import PartitionSpec as P

PIX = 32
EPS = 1e-6
WIN = 48
PITCH = 49
KDIM = 160
HALF = 256
MESH = pl.DeviceIdType.MESH


def window_table():
    table = np.zeros((512, 1024), np.float32)
    for py in range(2):
        for dx in range(4):
            for u in range(8):
                for v in range(16):
                    x = 2 * v + dx - 1
                    if 0 <= x < PIX:
                        table[(2 * u + py) * PIX + x, (py * 4 + dx) * 128 + u * 16 + v] = 1
    return table


def weight_table():
    table = np.zeros((81, 1024), np.float32)
    for py in range(2):
        for px in range(2):
            for t in range(3):
                for a in range(3):
                    for b in range(3):
                        for k in range(3):
                            col = t * WIN + ((a + py) * 4 + b + px) * 3 + k
                            table[t * 27 + (a * 3 + b) * 3 + k, (py * 2 + px) * 256 + col] = 1
    return table


def down_table():
    table = np.zeros((512, 512), np.float32)
    for c in range(128):
        for ab in range(4):
            table[4 * c + ab, ab * 128 + c] = 1
    return table


def place_table():
    px = np.arange(HALF)
    place = (px // 16 // 4) * 4 + (px % 16) // 4
    return (place[:, None] == (np.arange(256) % 16)[None, :]).astype(np.float32)


def head_table():
    table = np.zeros((256, 256), np.float32)
    for j in range(16):
        for ab in range(16):
            table[j * 16 + ab, ab * 16 + j] = 1
    return table


def iota(shape, axis):
    return lax.broadcasted_iota(jnp.int32, shape, axis)


def column(row):
    n = row.shape[1]
    same = iota((n, n), 0) == iota((n, n), 1)
    return jnp.sum(jnp.where(same, row, jnp.zeros((), row.dtype)), axis=1, keepdims=True)


def norm_silu(values, gain):
    mean_square = jnp.sum(values * values, axis=0, keepdims=True) * (1.0 / values.shape[0])
    half = (values * gain) * (0.5 * lax.rsqrt(mean_square + EPS))
    return (half + half * jnp.tanh(half)).astype(jnp.bfloat16)


def dot(a, b):
    return jnp.dot(a, b, preferred_element_type=jnp.float32)


def kernel(*refs):
    sources, (out_ref, *rest) = refs[:17], refs[17:]
    loaded, rest = rest[:17], rest[17:]
    (windows, w2, wd, heads, gin_s, gdown_s, bdown_s, parts, flags, enc, held, pick_s) = rest[:12]
    convolved, full, reduced = rest[12:15]
    load_sem, send_sem, recv_sem = rest[15:]
    loads = [
        pltpu.make_async_copy(source, target, load_sem.at[at])
        for at, (source, target) in enumerate(zip(sources, loaded))
    ]
    for load in loads:
        load.start()
    (
        lens_ref, readers_ref, owners_ref, frames_ref, wtab_ref, win_ref, bin_ref, gin_ref,
        wdown_ref, bdown_ref, gdown_ref, whead_ref, bhead_ref, etab_ref, dtab_ref, htab_ref,
        ptab_ref,
    ) = loaded
    me = lax.axis_index("wide")
    n, rows = held.shape[0], held.shape[1]
    barrier = pltpu.get_barrier_semaphore()
    for d in range(1, n):
        pl.semaphore_signal(
            barrier, inc=1, device_id={"wide": lax.rem(me + d, n)}, device_id_type=MESH
        )
    for load in loads[:5]:
        load.wait()
    read_rows = frames_ref.shape[0]
    most = read_rows // 4
    clips = lens_ref.shape[1]
    mine_at = me.astype(jnp.float32)
    len_row, reader_row, owner_row = (
        ref[...].astype(jnp.float32) for ref in (lens_ref, readers_ref, owners_ref)
    )
    len_col, reader_col, owner_col = column(len_row), column(reader_row), column(owner_row)
    earlier = iota((clips, clips), 1) < iota((clips, clips), 0)
    before_here = jnp.sum(
        jnp.where(earlier & (reader_row == reader_col), len_row, 0.0), axis=1, keepdims=True
    )
    first_len = jnp.sum(
        jnp.where((reader_col == mine_at) & (before_here == 0.0), len_col, 0.0),
        axis=0,
        keepdims=True,
    )

    last = 4 * most - 6
    row = iota((read_rows, 1), 0)
    number = ((row + 2) // 4 - 1).astype(jnp.float32)
    offset = ((row + 2) % 4).astype(jnp.float32)
    second = jnp.where(number >= first_len - 1.0, 1.0, 0.0)
    step = number + 1.0 - second * (first_len - 1.0)
    second_at = 4.0 * first_len - 3.0
    source = second * second_at + 4.0 * step - 3.0 + offset
    source = jnp.where(row < last, source, -1.0)
    source = jnp.where(row == 0, -1.0, source)
    source = jnp.where(row == 1, 0.0, source)
    source = jnp.where(row == last + 1, second_at, source)
    order = (iota((read_rows, read_rows), 1).astype(jnp.float32) == source).astype(jnp.bfloat16)
    frames = dot(order, frames_ref[...]).astype(jnp.bfloat16)
    flags[...] = jnp.where(
        iota(flags.shape, 0).astype(jnp.float32) == first_len - 1.0, 1.0, 0.0
    ) * jnp.ones(flags.shape, jnp.float32)

    stacked = jnp.concatenate(
        [
            frames[:, k * 1024 + h * 512 : k * 1024 + (h + 1) * 512]
            for k in range(3)
            for h in range(2)
        ],
        axis=0,
    )
    planes = dot(stacked, wtab_ref[...])
    lane = iota((read_rows, HALF), 1)
    for k in range(3):
        for dx in range(4):
            plane = []
            for py in range(2):
                at = (py * 4 + dx) * 128
                plane.append(
                    jnp.concatenate(
                        [
                            planes[
                                (2 * k + h) * read_rows : (2 * k + h + 1) * read_rows,
                                at : at + 128,
                            ]
                            for h in range(2)
                        ],
                        axis=1,
                    )
                )
            above = jnp.where(lane < 16, 0.0, pltpu.roll(plane[1], 16, 1))
            below = jnp.where(lane >= HALF - 16, 0.0, pltpu.roll(plane[0], HALF - 16, 1))
            for dy, value in enumerate((above, plane[0], plane[1], below)):
                row = (dy * 4 + dx) * 3 + k
                for h in range(2):
                    windows[h, pl.ds(row, read_rows, stride=PITCH), :] = value[
                        :, h * 128 : (h + 1) * 128
                    ]

    for load in loads[5:]:
        load.wait()
    spread = lax.dot_general(
        win_ref[...], etab_ref[...], (((0,), (0,)), ((), ())), preferred_element_type=jnp.float32
    )
    bias = column(bin_ref[...])
    high = bias.astype(jnp.bfloat16).astype(jnp.float32)
    mid = (bias - high).astype(jnp.bfloat16).astype(jnp.float32)
    low = bias - high - mid
    kcol = iota((128, KDIM), 1)
    tail = jnp.where(kcol == 3 * WIN, high, 0.0)
    tail = tail + jnp.where(kcol == 3 * WIN + 1, mid, 0.0)
    tail = tail + jnp.where(kcol == 3 * WIN + 2, low, 0.0)
    for ab in range(4):
        w2[ab * 128 : (ab + 1) * 128, :] = (
            spread[:, ab * 256 : ab * 256 + KDIM] + tail
        ).astype(jnp.bfloat16)
    wd[...] = dot(wdown_ref[...], dtab_ref[...]).astype(jnp.bfloat16)
    gin_s[...] = jnp.broadcast_to(column(gin_ref[...]), gin_s.shape)
    gdown_s[...] = jnp.broadcast_to(column(gdown_ref[...]), gdown_s.shape)
    bdown_s[...] = jnp.broadcast_to(column(bdown_ref[...]), bdown_s.shape)

    chunks = jnp.concatenate(
        [whead_ref[:, (s * 8 + c) * 256 : (s * 8 + c + 1) * 256] for c in range(8) for s in range(4)],
        axis=0,
    )
    turned = dot(chunks, htab_ref[...])
    piece = iota((64, 128), 1) // 16
    for ab in range(16):
        at = ab // 8 * 128
        row = jnp.zeros((64, 128), jnp.float32)
        for c in range(8):
            value = turned[c * 64 : (c + 1) * 64, at : at + 128]
            shift = (16 * c - ab % 8 * 16) % 128
            value = pltpu.roll(value, shift, 1) if shift else value
            row = jnp.where(piece == c, value, row)
        row = row.astype(jnp.bfloat16)
        for s in range(4):
            heads[ab * 16 : (ab + 1) * 16, s * 128 : (s + 1) * 128] = row[s * 16 : (s + 1) * 16]

    own_rows = out_ref.shape[0]
    own_off = jnp.sum(
        jnp.where(earlier & (owner_row == owner_col), len_row, 0.0), axis=1, keepdims=True
    )
    slot = iota((clips, 128), 1).astype(jnp.float32)
    place = slot - own_off
    inside = (owner_col == mine_at) & (place >= 0.0) & (place < len_col)
    late = before_here > 0.0
    opening = jnp.where(late, 1.0, 0.0)
    later = jnp.where(late, before_here, 1.0) + place
    source = reader_col * rows + jnp.where(place == 0.0, opening, later)
    picked = jnp.sum(jnp.where(inside, source + 1.0, 0.0), axis=0, keepdims=True) - 1.0
    pick = (iota((n * rows, 128), 0).astype(jnp.float32) == picked).astype(jnp.float32)
    pick_s[...] = pick.T.astype(jnp.bfloat16)

    ones = jnp.ones((KDIM - 3 * WIN, HALF), jnp.bfloat16)

    def window(slot):
        return jnp.concatenate(
            [windows[h, pl.ds(slot * PITCH, WIN), :] for h in range(2)], axis=1
        )

    def encode_frames(columns_of, count):
        for t in range(count + 2):
            cols = jnp.concatenate([columns_of(t), ones], axis=0) if t < count else None
            for part in range(2):
                at = part * 256
                if t < count:
                    convolved[t % 2, at : at + 256, :] = dot(w2[at : at + 256, :], cols)
                if 1 <= t <= count:
                    for row in (at, at + 128):
                        full[(t - 1) % 2, row : row + 128, :] = norm_silu(
                            convolved[(t - 1) % 2, row : row + 128, :], gin_s[...]
                        )
            if t >= 2:
                lowered = dot(wd[...], full[t % 2]) + bdown_s[...]
                reduced[(t - 2) * 128 : (t - 1) * 128, :] = norm_silu(lowered, gdown_s[...])

    pix = iota((16, HALF), 1)
    sub = ((pix // 16) % 4) * 4 + pix % 4

    def keep(spot, both):
        total = jnp.zeros((16, HALF), jnp.float32)
        for ab in range(16):
            total = total + jnp.where(sub == ab, both[ab * 16 : (ab + 1) * 16, :], 0.0)
        parts[pl.ds(pl.multiple_of(spot * 16, 16), 16), :] = total

    blank = jnp.zeros((2 * WIN, HALF), jnp.bfloat16)
    openings = (1, last + 1)
    encode_frames(
        lambda t: jnp.concatenate([blank, window(openings[t]).astype(jnp.bfloat16)], axis=0), 2
    )
    for spot in range(2):
        keep(spot, dot(heads[:, 384:512], reduced[spot * 128 : (spot + 1) * 128, :]))

    pair = 2 if most % 2 == 0 else 1

    def groups(at, carry):
        made = {}

        def columns_of(t):
            g = t // 4
            if g not in made:
                number = at * pair + g
                flag = flags[pl.ds(number, 1), :]
                slots = [
                    window(4 * number + s) * (1.0 - flag) + window(last + s) * flag
                    for s in range(2)
                ]
                slots += [window(4 * number + s) for s in range(2, 6)]
                made[g] = jnp.concatenate(slots, axis=0).astype(jnp.bfloat16)
            return made[g][t % 4 * WIN : (t % 4 + 3) * WIN, :]

        encode_frames(columns_of, 4 * pair)
        for g in range(pair):
            keep(at * pair + g + 2, dot(heads[...], reduced[g * 512 : (g + 1) * 512, :]))
        return carry

    lax.fori_loop(0, (most - 2) // pair, groups, 0)

    value = parts[...]
    top = value.astype(jnp.bfloat16)
    rest = (value - top.astype(jnp.float32)).astype(jnp.bfloat16)
    wide = dot(top, ptab_ref[...]) + dot(rest, ptab_ref[...])
    match = iota((most * 16, 256), 1) // 16 == iota((most * 16, 256), 0) % 16
    wide = jnp.where(match, wide, 0.0).reshape(most, 16, 256)
    bh = jnp.where(
        iota((16, 256), 1) // 16 == iota((16, 256), 0), column(bhead_ref[...]), 0.0
    )
    bh = jnp.sum(bh, axis=0, keepdims=True)
    result = jnp.sum(wide, axis=1) + bh
    if rows > most:
        result = jnp.concatenate([result, jnp.zeros((rows - most, 256), jnp.float32)], axis=0)
    enc[...] = result.astype(jnp.bfloat16)

    pl.semaphore_wait(barrier, n - 1)
    copies = []
    for d in range(1, n):
        copy = pltpu.make_async_remote_copy(
            src_ref=enc,
            dst_ref=held.at[me],
            send_sem=send_sem.at[d],
            recv_sem=recv_sem.at[d],
            device_id={"wide": lax.rem(me + d, n)},
            device_id_type=MESH,
        )
        copy.start()
        copies.append(copy)
    held[me] = enc[...]
    for copy in copies:
        copy.wait()
    result = dot(pick_s[...], held[...].reshape(n * rows, 256))
    out_ref[...] = result[:own_rows].astype(jnp.bfloat16)


def shards(
    frames, latent_len, reader, owner, w_in, b_in, g_in, w_down, b_down, g_down, w_head, b_head
):
    n = lax.axis_size("wide")
    read_rows = frames.shape[0]
    most = read_rows // 4
    held_rows = -(-most // 16) * 16
    own_rows = 2 * ((most + 2) // 2)
    hbm = pl.BlockSpec(memory_space=pltpu.HBM)
    vmem = pl.BlockSpec(memory_space=pltpu.VMEM)
    wtab, etab, dtab, htab, ptab = (
        jnp.asarray(t, dtype=jnp.bfloat16)
        for t in (window_table(), weight_table(), down_table(), head_table(), place_table())
    )
    operands = (
        latent_len[None, :], reader[None, :], owner[None, :], frames, wtab, w_in.T,
        b_in[None, :], g_in[None, :], w_down, b_down[None, :], g_down[None, :], w_head,
        b_head[None, :], etab, dtab, htab, ptab,
    )
    return pl.pallas_call(
        kernel,
        out_shape=jax.ShapeDtypeStruct((own_rows, 256), jnp.bfloat16),
        in_specs=[hbm] * len(operands),
        out_specs=vmem,
        scratch_shapes=[pltpu.VMEM(value.shape, value.dtype) for value in operands]
        + [
            pltpu.VMEM((2, read_rows * PITCH, 128), jnp.float32),
            pltpu.VMEM((512, KDIM), jnp.bfloat16),
            pltpu.VMEM((128, 512), jnp.bfloat16),
            pltpu.VMEM((256, 512), jnp.bfloat16),
            pltpu.VMEM((128, HALF), jnp.float32),
            pltpu.VMEM((128, HALF), jnp.float32),
            pltpu.VMEM((128, HALF), jnp.float32),
            pltpu.VMEM((most * 16, HALF), jnp.float32),
            pltpu.VMEM((most, HALF), jnp.float32),
            pltpu.VMEM((held_rows, 256), jnp.bfloat16),
            pltpu.VMEM((n, held_rows, 256), jnp.bfloat16),
            pltpu.VMEM((128, n * held_rows), jnp.bfloat16),
            pltpu.VMEM((2, 512, HALF), jnp.float32),
            pltpu.VMEM((2, 512, HALF), jnp.bfloat16),
            pltpu.VMEM((1024, HALF), jnp.bfloat16),
            pltpu.SemaphoreType.DMA((len(operands),)),
            pltpu.SemaphoreType.DMA((n,)),
            pltpu.SemaphoreType.DMA((n,)),
        ],
        compiler_params=pltpu.CompilerParams(
            collective_id=0, has_side_effects=True, vmem_limit_bytes=32 * 1024 * 1024
        ),
        name="encode",
    )(*operands)


def solution(mesh):
    return jax.shard_map(
        shards,
        mesh=mesh,
        in_specs=(
            P(("groups", "wide"), None),
            P("groups"),
            P("groups"),
            P("groups"),
            P(),
            P(),
            P(),
            P(),
            P(),
            P(),
            P(),
            P(),
        ),
        out_specs=P(("groups", "wide"), None),
        check_vma=False,
    )
```

```python
import functools

import jax
import jax.numpy as jnp
import numpy as np
from jax import lax
from jax.experimental import pallas as pl
from jax.experimental.pallas import tpu as pltpu
from jax.sharding import PartitionSpec as P

PIX = 32
EPS = 1e-6
WIN = 48
PITCH = 49
KDIM = 160
HALF = 256
MESH = pl.DeviceIdType.MESH


def window_table():
    table = np.zeros((512, 1024), np.float32)
    for py in range(2):
        for dx in range(4):
            for u in range(8):
                for v in range(16):
                    x = 2 * v + dx - 1
                    if 0 <= x < PIX:
                        table[(2 * u + py) * PIX + x, (py * 4 + dx) * 128 + u * 16 + v] = 1
    return table


def weight_table():
    table = np.zeros((81, 1024), np.float32)
    for py in range(2):
        for px in range(2):
            for t in range(3):
                for a in range(3):
                    for b in range(3):
                        for k in range(3):
                            col = t * WIN + ((a + py) * 4 + b + px) * 3 + k
                            table[t * 27 + (a * 3 + b) * 3 + k, (py * 2 + px) * 256 + col] = 1
    return table


def down_table():
    table = np.zeros((512, 512), np.float32)
    for c in range(128):
        for ab in range(4):
            table[4 * c + ab, ab * 128 + c] = 1
    return table


def place_table():
    px = np.arange(HALF)
    place = (px // 16 // 4) * 4 + (px % 16) // 4
    return (place[:, None] == (np.arange(256) % 16)[None, :]).astype(np.float32)


def head_table():
    table = np.zeros((256, 256), np.float32)
    for j in range(16):
        for ab in range(16):
            table[j * 16 + ab, ab * 16 + j] = 1
    return table


def iota(shape, axis):
    return lax.broadcasted_iota(jnp.int32, shape, axis)


def column(row):
    n = row.shape[1]
    same = iota((n, n), 0) == iota((n, n), 1)
    return jnp.sum(jnp.where(same, row, jnp.zeros((), row.dtype)), axis=1, keepdims=True)


def norm_silu(values, gain):
    mean_square = jnp.sum(values * values, axis=0, keepdims=True) * (1.0 / values.shape[0])
    half = (values * gain) * (0.5 * lax.rsqrt(mean_square + EPS))
    return (half + half * jnp.tanh(half)).astype(jnp.bfloat16)


def dot(a, b):
    return jnp.dot(a, b, preferred_element_type=jnp.float32)


def kernel(*refs):
    sources, (out_ref, *rest) = refs[:17], refs[17:]
    loaded, rest = rest[:17], rest[17:]
    (windows, w2, wd, heads, gin_s, gdown_s, bdown_s, parts, flags, enc, held, pick_s) = rest[:12]
    convolved, full, reduced = rest[12:15]
    load_sem, send_sem, recv_sem = rest[15:]
    loads = [
        pltpu.make_async_copy(source, target, load_sem.at[at])
        for at, (source, target) in enumerate(zip(sources, loaded))
    ]
    for load in loads:
        load.start()
    (
        lens_ref, readers_ref, owners_ref, frames_ref, wtab_ref, win_ref, bin_ref, gin_ref,
        wdown_ref, bdown_ref, gdown_ref, whead_ref, bhead_ref, etab_ref, dtab_ref, htab_ref,
        ptab_ref,
    ) = loaded
    me = lax.axis_index("wide")
    n, rows = held.shape[0], held.shape[1]
    barrier = pltpu.get_barrier_semaphore()
    for d in range(1, n):
        pl.semaphore_signal(
            barrier, inc=1, device_id={"wide": lax.rem(me + d, n)}, device_id_type=MESH
        )
    for load in loads[:5]:
        load.wait()
    read_rows = frames_ref.shape[0]
    most = read_rows // 4
    clips = lens_ref.shape[1]
    mine_at = me.astype(jnp.float32)
    len_row, reader_row, owner_row = (
        ref[...].astype(jnp.float32) for ref in (lens_ref, readers_ref, owners_ref)
    )
    len_col, reader_col, owner_col = column(len_row), column(reader_row), column(owner_row)
    earlier = iota((clips, clips), 1) < iota((clips, clips), 0)
    before_here = jnp.sum(
        jnp.where(earlier & (reader_row == reader_col), len_row, 0.0), axis=1, keepdims=True
    )
    first_len = jnp.sum(
        jnp.where((reader_col == mine_at) & (before_here == 0.0), len_col, 0.0),
        axis=0,
        keepdims=True,
    )

    last = 4 * most - 6
    row = iota((read_rows, 1), 0)
    number = ((row + 2) // 4 - 1).astype(jnp.float32)
    offset = ((row + 2) % 4).astype(jnp.float32)
    second = jnp.where(number >= first_len - 1.0, 1.0, 0.0)
    step = number + 1.0 - second * (first_len - 1.0)
    second_at = 4.0 * first_len - 3.0
    source = second * second_at + 4.0 * step - 3.0 + offset
    source = jnp.where(row < last, source, -1.0)
    source = jnp.where(row == 0, -1.0, source)
    source = jnp.where(row == 1, 0.0, source)
    source = jnp.where(row == last + 1, second_at, source)
    order = (iota((read_rows, read_rows), 1).astype(jnp.float32) == source).astype(jnp.bfloat16)
    frames = dot(order, frames_ref[...]).astype(jnp.bfloat16)
    flags[...] = jnp.where(
        iota(flags.shape, 0).astype(jnp.float32) == first_len - 1.0, 1.0, 0.0
    ) * jnp.ones(flags.shape, jnp.float32)

    stacked = jnp.concatenate(
        [
            frames[:, k * 1024 + h * 512 : k * 1024 + (h + 1) * 512]
            for k in range(3)
            for h in range(2)
        ],
        axis=0,
    )
    planes = dot(stacked, wtab_ref[...])
    lane = iota((read_rows, HALF), 1)
    for k in range(3):
        for dx in range(4):
            plane = []
            for py in range(2):
                at = (py * 4 + dx) * 128
                plane.append(
                    jnp.concatenate(
                        [
                            planes[
                                (2 * k + h) * read_rows : (2 * k + h + 1) * read_rows,
                                at : at + 128,
                            ]
                            for h in range(2)
                        ],
                        axis=1,
                    )
                )
            above = jnp.where(lane < 16, 0.0, pltpu.roll(plane[1], 16, 1))
            below = jnp.where(lane >= HALF - 16, 0.0, pltpu.roll(plane[0], HALF - 16, 1))
            for dy, value in enumerate((above, plane[0], plane[1], below)):
                row = (dy * 4 + dx) * 3 + k
                for h in range(2):
                    windows[h, pl.ds(row, read_rows, stride=PITCH), :] = value[
                        :, h * 128 : (h + 1) * 128
                    ]

    for load in loads[5:]:
        load.wait()
    spread = lax.dot_general(
        win_ref[...], etab_ref[...], (((0,), (0,)), ((), ())), preferred_element_type=jnp.float32
    )
    bias = column(bin_ref[...])
    high = bias.astype(jnp.bfloat16).astype(jnp.float32)
    mid = (bias - high).astype(jnp.bfloat16).astype(jnp.float32)
    low = bias - high - mid
    kcol = iota((128, KDIM), 1)
    tail = jnp.where(kcol == 3 * WIN, high, 0.0)
    tail = tail + jnp.where(kcol == 3 * WIN + 1, mid, 0.0)
    tail = tail + jnp.where(kcol == 3 * WIN + 2, low, 0.0)
    for ab in range(4):
        w2[ab * 128 : (ab + 1) * 128, :] = (
            spread[:, ab * 256 : ab * 256 + KDIM] + tail
        ).astype(jnp.bfloat16)
    wd[...] = dot(wdown_ref[...], dtab_ref[...]).astype(jnp.bfloat16)
    gin_s[...] = jnp.broadcast_to(column(gin_ref[...]), gin_s.shape)
    gdown_s[...] = jnp.broadcast_to(column(gdown_ref[...]), gdown_s.shape)
    bdown_s[...] = jnp.broadcast_to(column(bdown_ref[...]), bdown_s.shape)

    chunks = jnp.concatenate(
        [whead_ref[:, (s * 8 + c) * 256 : (s * 8 + c + 1) * 256] for c in range(8) for s in range(4)],
        axis=0,
    )
    turned = dot(chunks, htab_ref[...])
    piece = iota((64, 128), 1) // 16
    for ab in range(16):
        at = ab // 8 * 128
        row = jnp.zeros((64, 128), jnp.float32)
        for c in range(8):
            value = turned[c * 64 : (c + 1) * 64, at : at + 128]
            shift = (16 * c - ab % 8 * 16) % 128
            value = pltpu.roll(value, shift, 1) if shift else value
            row = jnp.where(piece == c, value, row)
        row = row.astype(jnp.bfloat16)
        for s in range(4):
            heads[ab * 16 : (ab + 1) * 16, s * 128 : (s + 1) * 128] = row[s * 16 : (s + 1) * 16]

    own_rows = out_ref.shape[0]
    own_off = jnp.sum(
        jnp.where(earlier & (owner_row == owner_col), len_row, 0.0), axis=1, keepdims=True
    )
    slot = iota((clips, 128), 1).astype(jnp.float32)
    place = slot - own_off
    inside = (owner_col == mine_at) & (place >= 0.0) & (place < len_col)
    late = before_here > 0.0
    opening = jnp.where(late, 1.0, 0.0)
    later = jnp.where(late, before_here, 1.0) + place
    source = reader_col * rows + jnp.where(place == 0.0, opening, later)
    picked = jnp.sum(jnp.where(inside, source + 1.0, 0.0), axis=0, keepdims=True) - 1.0
    pick = (iota((n * rows, 128), 0).astype(jnp.float32) == picked).astype(jnp.float32)
    pick_s[...] = pick.T.astype(jnp.bfloat16)

    ones = jnp.ones((KDIM - 3 * WIN, HALF), jnp.bfloat16)

    def window(slot):
        return jnp.concatenate(
            [windows[h, pl.ds(slot * PITCH, WIN), :] for h in range(2)], axis=1
        )

    def stage(cols, odd, spot):
        if cols is not None:
            cols = jnp.concatenate([cols, ones], axis=0)
        for part in range(2):
            at = part * 256
            if cols is not None:
                convolved[odd, at : at + 256, :] = dot(w2[at : at + 256, :], cols)
            for row in (at, at + 128):
                full[1 - odd, row : row + 128, :] = norm_silu(
                    convolved[1 - odd, row : row + 128, :], gin_s[...]
                )
        if spot is not None:
            second_product(odd, spot)

    def second_product(odd, spot):
        lowered = dot(wd[...], full[odd]) + bdown_s[...]
        reduced[spot * 128 : (spot + 1) * 128, :] = norm_silu(lowered, gdown_s[...])

    pix = iota((16, HALF), 1)
    sub = ((pix // 16) % 4) * 4 + pix % 4

    def keep(spot, both):
        total = jnp.zeros((16, HALF), jnp.float32)
        for ab in range(16):
            total = total + jnp.where(sub == ab, both[ab * 16 : (ab + 1) * 16, :], 0.0)
        parts[pl.ds(pl.multiple_of(spot * 16, 16), 16), :] = total

    def opening(at):
        blank = jnp.zeros((2 * WIN, HALF), jnp.bfloat16)
        return jnp.concatenate([blank, window(at).astype(jnp.bfloat16)], axis=0)

    def group_columns(at):
        flag = flags[pl.ds(at, 1), :]
        slots = [
            window(4 * at + s) * (1.0 - flag) + window(last + s) * flag for s in range(2)
        ]
        slots += [window(4 * at + s) for s in range(2, 6)]
        cols = jnp.concatenate(slots, axis=0).astype(jnp.bfloat16)
        return [cols[s * WIN : (s + 3) * WIN, :] for s in range(4)]

    first = jnp.concatenate([opening(1), ones], axis=0)
    convolved[0] = dot(w2[...], first)
    stage(opening(last + 1), 1, None)
    cols = group_columns(0)
    stage(cols[0], 0, 2)
    keep(0, dot(heads[:, 384:512], reduced[256:384, :]))
    stage(cols[1], 1, 3)
    keep(1, dot(heads[:, 384:512], reduced[384:512, :]))
    stage(cols[2], 0, 0)
    stage(cols[3], 1, 1)

    def group(at, carry):
        cols = group_columns(at)
        stage(cols[0], 0, 2)
        stage(cols[1], 1, 3)
        keep(at + 1, dot(heads[...], reduced[...]))
        stage(cols[2], 0, 0)
        stage(cols[3], 1, 1)
        return carry

    lax.fori_loop(1, most - 2, group, 0)
    stage(None, 0, 2)
    second_product(1, 3)
    keep(most - 1, dot(heads[...], reduced[...]))

    value = parts[...]
    top = value.astype(jnp.bfloat16)
    rest = (value - top.astype(jnp.float32)).astype(jnp.bfloat16)
    wide = dot(top, ptab_ref[...]) + dot(rest, ptab_ref[...])
    match = iota((most * 16, 256), 1) // 16 == iota((most * 16, 256), 0) % 16
    wide = jnp.where(match, wide, 0.0).reshape(most, 16, 256)
    bh = jnp.where(
        iota((16, 256), 1) // 16 == iota((16, 256), 0), column(bhead_ref[...]), 0.0
    )
    bh = jnp.sum(bh, axis=0, keepdims=True)
    result = jnp.sum(wide, axis=1) + bh
    if rows > most:
        result = jnp.concatenate([result, jnp.zeros((rows - most, 256), jnp.float32)], axis=0)
    enc[...] = result.astype(jnp.bfloat16)

    pl.semaphore_wait(barrier, n - 1)
    copies = []
    for d in range(1, n):
        copy = pltpu.make_async_remote_copy(
            src_ref=enc,
            dst_ref=held.at[me],
            send_sem=send_sem.at[d],
            recv_sem=recv_sem.at[d],
            device_id={"wide": lax.rem(me + d, n)},
            device_id_type=MESH,
        )
        copy.start()
        copies.append(copy)
    held[me] = enc[...]
    for copy in copies:
        copy.wait()
    result = dot(pick_s[...], held[...].reshape(n * rows, 256))
    out_ref[...] = result[:own_rows].astype(jnp.bfloat16)


def shards(
    frames, latent_len, reader, owner, w_in, b_in, g_in, w_down, b_down, g_down, w_head, b_head
):
    n = lax.axis_size("wide")
    read_rows = frames.shape[0]
    most = read_rows // 4
    held_rows = -(-most // 16) * 16
    own_rows = 2 * ((most + 2) // 2)
    hbm = pl.BlockSpec(memory_space=pltpu.HBM)
    vmem = pl.BlockSpec(memory_space=pltpu.VMEM)
    wtab, etab, dtab, htab, ptab = (
        jnp.asarray(t, dtype=jnp.bfloat16)
        for t in (window_table(), weight_table(), down_table(), head_table(), place_table())
    )
    operands = (
        latent_len[None, :], reader[None, :], owner[None, :], frames, wtab, w_in.T,
        b_in[None, :], g_in[None, :], w_down, b_down[None, :], g_down[None, :], w_head,
        b_head[None, :], etab, dtab, htab, ptab,
    )
    return pl.pallas_call(
        kernel,
        out_shape=jax.ShapeDtypeStruct((own_rows, 256), jnp.bfloat16),
        in_specs=[hbm] * len(operands),
        out_specs=vmem,
        scratch_shapes=[pltpu.VMEM(value.shape, value.dtype) for value in operands]
        + [
            pltpu.VMEM((2, read_rows * PITCH, 128), jnp.float32),
            pltpu.VMEM((512, KDIM), jnp.bfloat16),
            pltpu.VMEM((128, 512), jnp.bfloat16),
            pltpu.VMEM((256, 512), jnp.bfloat16),
            pltpu.VMEM((128, HALF), jnp.float32),
            pltpu.VMEM((128, HALF), jnp.float32),
            pltpu.VMEM((128, HALF), jnp.float32),
            pltpu.VMEM((most * 16, HALF), jnp.float32),
            pltpu.VMEM((most, HALF), jnp.float32),
            pltpu.VMEM((held_rows, 256), jnp.bfloat16),
            pltpu.VMEM((n, held_rows, 256), jnp.bfloat16),
            pltpu.VMEM((128, n * held_rows), jnp.bfloat16),
            pltpu.VMEM((2, 512, HALF), jnp.float32),
            pltpu.VMEM((2, 512, HALF), jnp.bfloat16),
            pltpu.VMEM((512, HALF), jnp.bfloat16),
            pltpu.SemaphoreType.DMA((len(operands),)),
            pltpu.SemaphoreType.DMA((n,)),
            pltpu.SemaphoreType.DMA((n,)),
        ],
        compiler_params=pltpu.CompilerParams(
            collective_id=0, has_side_effects=True, vmem_limit_bytes=56 * 1024 * 1024
        ),
        name="encode",
    )(*operands)


def solution(mesh):
    return jax.shard_map(
        shards,
        mesh=mesh,
        in_specs=(
            P(("groups", "wide"), None),
            P("groups"),
            P("groups"),
            P("groups"),
            P(),
            P(),
            P(),
            P(),
            P(),
            P(),
            P(),
            P(),
        ),
        out_specs=P(("groups", "wide"), None),
        check_vma=False,
    )
```

```python
import functools

import jax
import jax.numpy as jnp
import numpy as np
from jax import lax
from jax.experimental import pallas as pl
from jax.experimental.pallas import tpu as pltpu
from jax.sharding import PartitionSpec as P

PIX = 32
EPS = 1e-6
WIN = 48
PITCH = 49
KDIM = 160
HALF = 256
MESH = pl.DeviceIdType.MESH


def window_table():
    table = np.zeros((512, 1024), np.float32)
    for py in range(2):
        for dx in range(4):
            for u in range(8):
                for v in range(16):
                    x = 2 * v + dx - 1
                    if 0 <= x < PIX:
                        table[(2 * u + py) * PIX + x, (py * 4 + dx) * 128 + u * 16 + v] = 1
    return table


def weight_table():
    table = np.zeros((81, 1024), np.float32)
    for py in range(2):
        for px in range(2):
            for t in range(3):
                for a in range(3):
                    for b in range(3):
                        for k in range(3):
                            col = t * WIN + ((a + py) * 4 + b + px) * 3 + k
                            table[t * 27 + (a * 3 + b) * 3 + k, (py * 2 + px) * 256 + col] = 1
    return table


def down_table():
    table = np.zeros((512, 512), np.float32)
    for c in range(128):
        for ab in range(4):
            table[4 * c + ab, ab * 128 + c] = 1
    return table


def place_table():
    px = np.arange(HALF)
    place = (px // 16 // 4) * 4 + (px % 16) // 4
    return (place[:, None] == (np.arange(256) % 16)[None, :]).astype(np.float32)


def head_table():
    table = np.zeros((256, 256), np.float32)
    for j in range(16):
        for ab in range(16):
            table[j * 16 + ab, ab * 16 + j] = 1
    return table


def iota(shape, axis):
    return lax.broadcasted_iota(jnp.int32, shape, axis)


def column(row):
    n = row.shape[1]
    same = iota((n, n), 0) == iota((n, n), 1)
    return jnp.sum(jnp.where(same, row, jnp.zeros((), row.dtype)), axis=1, keepdims=True)


def norm_silu(values, gain):
    mean_square = jnp.sum(values * values, axis=0, keepdims=True) * (1.0 / values.shape[0])
    half = (values * gain) * (0.5 * lax.rsqrt(mean_square + EPS))
    return (half + half * jnp.tanh(half)).astype(jnp.bfloat16)


def dot(a, b):
    return jnp.dot(a, b, preferred_element_type=jnp.float32)


def kernel(*refs):
    sources, (out_ref, *rest) = refs[:17], refs[17:]
    loaded, rest = rest[:17], rest[17:]
    (windows, w2, wd, heads, gin_s, gdown_s, bdown_s, parts, flags, enc, held, pick_s) = rest[:12]
    convolved, full, reduced = rest[12:15]
    load_sem, send_sem, recv_sem = rest[15:]
    loads = [
        pltpu.make_async_copy(source, target, load_sem.at[at])
        for at, (source, target) in enumerate(zip(sources, loaded))
    ]
    for load in loads:
        load.start()
    (
        lens_ref, readers_ref, owners_ref, frames_ref, wtab_ref, win_ref, bin_ref, gin_ref,
        wdown_ref, bdown_ref, gdown_ref, whead_ref, bhead_ref, etab_ref, dtab_ref, htab_ref,
        ptab_ref,
    ) = loaded
    me = lax.axis_index("wide")
    n, rows = held.shape[0], held.shape[1]
    barrier = pltpu.get_barrier_semaphore()
    for d in range(1, n):
        pl.semaphore_signal(
            barrier, inc=1, device_id={"wide": lax.rem(me + d, n)}, device_id_type=MESH
        )
    for load in loads[:5]:
        load.wait()
    read_rows = frames_ref.shape[0]
    most = read_rows // 4
    clips = lens_ref.shape[1]
    mine_at = me.astype(jnp.float32)
    len_row, reader_row, owner_row = (
        ref[...].astype(jnp.float32) for ref in (lens_ref, readers_ref, owners_ref)
    )
    len_col, reader_col, owner_col = column(len_row), column(reader_row), column(owner_row)
    earlier = iota((clips, clips), 1) < iota((clips, clips), 0)
    before_here = jnp.sum(
        jnp.where(earlier & (reader_row == reader_col), len_row, 0.0), axis=1, keepdims=True
    )
    first_len = jnp.sum(
        jnp.where((reader_col == mine_at) & (before_here == 0.0), len_col, 0.0),
        axis=0,
        keepdims=True,
    )

    last = 4 * most - 6
    row = iota((read_rows, 1), 0)
    number = ((row + 2) // 4 - 1).astype(jnp.float32)
    offset = ((row + 2) % 4).astype(jnp.float32)
    second = jnp.where(number >= first_len - 1.0, 1.0, 0.0)
    step = number + 1.0 - second * (first_len - 1.0)
    second_at = 4.0 * first_len - 3.0
    source = second * second_at + 4.0 * step - 3.0 + offset
    source = jnp.where(row < last, source, -1.0)
    source = jnp.where(row == 0, -1.0, source)
    source = jnp.where(row == 1, 0.0, source)
    source = jnp.where(row == last + 1, second_at, source)
    order = (iota((read_rows, read_rows), 1).astype(jnp.float32) == source).astype(jnp.bfloat16)
    frames = dot(order, frames_ref[...]).astype(jnp.bfloat16)
    flags[...] = jnp.where(
        iota(flags.shape, 0).astype(jnp.float32) == first_len - 1.0, 1.0, 0.0
    ) * jnp.ones(flags.shape, jnp.float32)

    stacked = jnp.concatenate(
        [
            frames[:, k * 1024 + h * 512 : k * 1024 + (h + 1) * 512]
            for k in range(3)
            for h in range(2)
        ],
        axis=0,
    )
    planes = dot(stacked, wtab_ref[...])
    lane = iota((read_rows, HALF), 1)
    for k in range(3):
        for dx in range(4):
            plane = []
            for py in range(2):
                at = (py * 4 + dx) * 128
                plane.append(
                    jnp.concatenate(
                        [
                            planes[
                                (2 * k + h) * read_rows : (2 * k + h + 1) * read_rows,
                                at : at + 128,
                            ]
                            for h in range(2)
                        ],
                        axis=1,
                    )
                )
            above = jnp.where(lane < 16, 0.0, pltpu.roll(plane[1], 16, 1))
            below = jnp.where(lane >= HALF - 16, 0.0, pltpu.roll(plane[0], HALF - 16, 1))
            for dy, value in enumerate((above, plane[0], plane[1], below)):
                row = (dy * 4 + dx) * 3 + k
                for h in range(2):
                    windows[h, pl.ds(row, read_rows, stride=PITCH), :] = value[
                        :, h * 128 : (h + 1) * 128
                    ]

    for load in loads[5:]:
        load.wait()
    spread = lax.dot_general(
        win_ref[...], etab_ref[...], (((0,), (0,)), ((), ())), preferred_element_type=jnp.float32
    )
    bias = column(bin_ref[...])
    high = bias.astype(jnp.bfloat16).astype(jnp.float32)
    mid = (bias - high).astype(jnp.bfloat16).astype(jnp.float32)
    low = bias - high - mid
    kcol = iota((128, KDIM), 1)
    tail = jnp.where(kcol == 3 * WIN, high, 0.0)
    tail = tail + jnp.where(kcol == 3 * WIN + 1, mid, 0.0)
    tail = tail + jnp.where(kcol == 3 * WIN + 2, low, 0.0)
    for ab in range(4):
        w2[ab * 128 : (ab + 1) * 128, :] = (
            spread[:, ab * 256 : ab * 256 + KDIM] + tail
        ).astype(jnp.bfloat16)
    wd[...] = dot(wdown_ref[...], dtab_ref[...]).astype(jnp.bfloat16)
    gin_s[...] = jnp.broadcast_to(column(gin_ref[...]), gin_s.shape)
    gdown_s[...] = jnp.broadcast_to(column(gdown_ref[...]), gdown_s.shape)
    bdown_s[...] = jnp.broadcast_to(column(bdown_ref[...]), bdown_s.shape)

    chunks = jnp.concatenate(
        [whead_ref[:, (s * 8 + c) * 256 : (s * 8 + c + 1) * 256] for c in range(8) for s in range(4)],
        axis=0,
    )
    turned = dot(chunks, htab_ref[...])
    piece = iota((64, 128), 1) // 16
    for ab in range(16):
        at = ab // 8 * 128
        row = jnp.zeros((64, 128), jnp.float32)
        for c in range(8):
            value = turned[c * 64 : (c + 1) * 64, at : at + 128]
            shift = (16 * c - ab % 8 * 16) % 128
            value = pltpu.roll(value, shift, 1) if shift else value
            row = jnp.where(piece == c, value, row)
        row = row.astype(jnp.bfloat16)
        for s in range(4):
            heads[ab * 16 : (ab + 1) * 16, s * 128 : (s + 1) * 128] = row[s * 16 : (s + 1) * 16]

    own_off = jnp.sum(
        jnp.where(earlier & (owner_row == owner_col), len_row, 0.0), axis=1, keepdims=True
    )
    slot = iota((clips, 128), 1).astype(jnp.float32)
    place = slot - own_off
    inside = (owner_col == mine_at) & (place >= 0.0) & (place < len_col)
    late = before_here > 0.0
    opening = jnp.where(late, 1.0, 0.0)
    later = jnp.where(late, before_here, 1.0) + place
    source = reader_col * rows + jnp.where(place == 0.0, opening, later)
    picked = jnp.sum(jnp.where(inside, source + 1.0, 0.0), axis=0, keepdims=True) - 1.0
    pick = (iota((n * rows, 128), 0).astype(jnp.float32) == picked).astype(jnp.float32)
    pick_s[...] = pick.T.astype(jnp.bfloat16)

    ones = jnp.ones((KDIM - 3 * WIN, HALF), jnp.bfloat16)

    def window(slot):
        return jnp.concatenate(
            [windows[h, pl.ds(slot * PITCH, WIN), :] for h in range(2)], axis=1
        )

    def stage(cols, odd, spot):
        if cols is not None:
            convolved[odd] = dot(w2[...], jnp.concatenate([cols, ones], axis=0))
        for row in range(0, 512, 128):
            full[1 - odd, row : row + 128, :] = norm_silu(
                convolved[1 - odd, row : row + 128, :], gin_s[...]
            )
        if spot is not None:
            second_product(odd, spot)

    def second_product(odd, spot):
        lowered = dot(wd[...], full[odd]) + bdown_s[...]
        reduced[spot * 128 : (spot + 1) * 128, :] = norm_silu(lowered, gdown_s[...])

    pix = iota((16, HALF), 1)
    sub = ((pix // 16) % 4) * 4 + pix % 4

    def keep(spot, both):
        total = jnp.zeros((16, HALF), jnp.float32)
        for ab in range(16):
            total = total + jnp.where(sub == ab, both[ab * 16 : (ab + 1) * 16, :], 0.0)
        parts[pl.ds(pl.multiple_of(spot * 16, 16), 16), :] = total

    def opening(at):
        blank = jnp.zeros((2 * WIN, HALF), jnp.bfloat16)
        return jnp.concatenate([blank, window(at).astype(jnp.bfloat16)], axis=0)

    def group_columns(at):
        flag = flags[pl.ds(at, 1), :]
        slots = [
            window(4 * at + s) * (1.0 - flag) + window(last + s) * flag for s in range(2)
        ]
        slots += [window(4 * at + s) for s in range(2, 6)]
        cols = jnp.concatenate(slots, axis=0).astype(jnp.bfloat16)
        return [cols[s * WIN : (s + 3) * WIN, :] for s in range(4)]

    first = jnp.concatenate([opening(1), ones], axis=0)
    convolved[0] = dot(w2[...], first)
    stage(opening(last + 1), 1, None)
    cols = group_columns(0)
    stage(cols[0], 0, 2)
    keep(0, dot(heads[:, 384:512], reduced[256:384, :]))
    stage(cols[1], 1, 3)
    keep(1, dot(heads[:, 384:512], reduced[384:512, :]))
    stage(cols[2], 0, 0)
    stage(cols[3], 1, 1)

    def group(at, carry):
        cols = group_columns(at)
        stage(cols[0], 0, 2)
        stage(cols[1], 1, 3)
        keep(at + 1, dot(heads[...], reduced[...]))
        stage(cols[2], 0, 0)
        stage(cols[3], 1, 1)
        return carry

    lax.fori_loop(1, most - 2, group, 0)
    stage(None, 0, 2)
    second_product(1, 3)
    keep(most - 1, dot(heads[...], reduced[...]))

    value = parts[...]
    top = value.astype(jnp.bfloat16)
    rest = (value - top.astype(jnp.float32)).astype(jnp.bfloat16)
    wide = dot(top, ptab_ref[...]) + dot(rest, ptab_ref[...])
    match = iota((most * 16, 256), 1) // 16 == iota((most * 16, 256), 0) % 16
    wide = jnp.where(match, wide, 0.0).reshape(most, 16, 256)
    bh = jnp.where(
        iota((16, 256), 1) // 16 == iota((16, 256), 0), column(bhead_ref[...]), 0.0
    )
    bh = jnp.sum(bh, axis=0, keepdims=True)
    result = jnp.sum(wide, axis=1) + bh
    if rows > most:
        result = jnp.concatenate([result, jnp.zeros((rows - most, 256), jnp.float32)], axis=0)
    enc[...] = result.astype(jnp.bfloat16)

    pl.semaphore_wait(barrier, n - 1)
    copies = []
    for d in range(1, n):
        copy = pltpu.make_async_remote_copy(
            src_ref=enc,
            dst_ref=held.at[me],
            send_sem=send_sem.at[d],
            recv_sem=recv_sem.at[d],
            device_id={"wide": lax.rem(me + d, n)},
            device_id_type=MESH,
        )
        copy.start()
        copies.append(copy)
    held[me] = enc[...]
    for copy in copies:
        copy.wait()
    result = dot(pick_s[...], held[...].reshape(n * rows, 256))
    out_ref[...] = result[: out_ref.shape[0]]


def shards(
    frames, latent_len, reader, owner, w_in, b_in, g_in, w_down, b_down, g_down, w_head, b_head
):
    n = lax.axis_size("wide")
    read_rows = frames.shape[0]
    most = read_rows // 4
    held_rows = -(-most // 16) * 16
    own_rows = 2 * ((most + 2) // 2)
    hbm = pl.BlockSpec(memory_space=pltpu.HBM)
    vmem = pl.BlockSpec(memory_space=pltpu.VMEM)
    wtab, etab, dtab, htab, ptab = (
        jnp.asarray(t, dtype=jnp.bfloat16)
        for t in (window_table(), weight_table(), down_table(), head_table(), place_table())
    )
    operands = (
        latent_len[None, :], reader[None, :], owner[None, :], frames, wtab, w_in.T,
        b_in[None, :], g_in[None, :], w_down, b_down[None, :], g_down[None, :], w_head,
        b_head[None, :], etab, dtab, htab, ptab,
    )
    picked = pl.pallas_call(
        kernel,
        out_shape=jax.ShapeDtypeStruct((-(-own_rows // 8) * 8, 256), jnp.float32),
        in_specs=[hbm] * len(operands),
        out_specs=vmem,
        scratch_shapes=[pltpu.VMEM(value.shape, value.dtype) for value in operands]
        + [
            pltpu.VMEM((2, read_rows * PITCH, 128), jnp.float32),
            pltpu.VMEM((512, KDIM), jnp.bfloat16),
            pltpu.VMEM((128, 512), jnp.bfloat16),
            pltpu.VMEM((256, 512), jnp.bfloat16),
            pltpu.VMEM((128, HALF), jnp.float32),
            pltpu.VMEM((128, HALF), jnp.float32),
            pltpu.VMEM((128, HALF), jnp.float32),
            pltpu.VMEM((most * 16, HALF), jnp.float32),
            pltpu.VMEM((most, HALF), jnp.float32),
            pltpu.VMEM((held_rows, 256), jnp.bfloat16),
            pltpu.VMEM((n, held_rows, 256), jnp.bfloat16),
            pltpu.VMEM((128, n * held_rows), jnp.bfloat16),
            pltpu.VMEM((2, 512, HALF), jnp.float32),
            pltpu.VMEM((2, 512, HALF), jnp.bfloat16),
            pltpu.VMEM((512, HALF), jnp.bfloat16),
            pltpu.SemaphoreType.DMA((len(operands),)),
            pltpu.SemaphoreType.DMA((n,)),
            pltpu.SemaphoreType.DMA((n,)),
        ],
        compiler_params=pltpu.CompilerParams(
            collective_id=0, has_side_effects=True, vmem_limit_bytes=56 * 1024 * 1024
        ),
        name="encode",
    )(*operands)
    return picked[:own_rows].astype(jnp.bfloat16)


def solution(mesh):
    return jax.shard_map(
        shards,
        mesh=mesh,
        in_specs=(
            P(("groups", "wide"), None),
            P("groups"),
            P("groups"),
            P("groups"),
            P(),
            P(),
            P(),
            P(),
            P(),
            P(),
            P(),
            P(),
        ),
        out_specs=P(("groups", "wide"), None),
        check_vma=False,
    )
```

```python
import functools

import jax
import jax.numpy as jnp
import numpy as np
from jax import lax
from jax.experimental import pallas as pl
from jax.experimental.pallas import tpu as pltpu
from jax.sharding import PartitionSpec as P

PIX = 32
EPS = 1e-6
WIN = 48
PITCH = 49
KDIM = 160
HALF = 256
MESH = pl.DeviceIdType.MESH


def window_table():
    table = np.zeros((512, 1024), np.float32)
    for py in range(2):
        for dx in range(4):
            for u in range(8):
                for v in range(16):
                    x = 2 * v + dx - 1
                    if 0 <= x < PIX:
                        table[(2 * u + py) * PIX + x, (py * 4 + dx) * 128 + u * 16 + v] = 1
    return table


def weight_table():
    table = np.zeros((81, 1024), np.float32)
    for py in range(2):
        for px in range(2):
            for t in range(3):
                for a in range(3):
                    for b in range(3):
                        for k in range(3):
                            col = t * WIN + ((a + py) * 4 + b + px) * 3 + k
                            table[t * 27 + (a * 3 + b) * 3 + k, (py * 2 + px) * 256 + col] = 1
    return table


def down_table():
    table = np.zeros((512, 512), np.float32)
    for c in range(128):
        for ab in range(4):
            table[4 * c + ab, ab * 128 + c] = 1
    return table


def place_table():
    px = np.arange(HALF)
    place = (px // 16 // 4) * 4 + (px % 16) // 4
    return (place[:, None] == (np.arange(256) % 16)[None, :]).astype(np.float32)


def head_table():
    table = np.zeros((256, 256), np.float32)
    for j in range(16):
        for ab in range(16):
            table[j * 16 + ab, ab * 16 + j] = 1
    return table


def iota(shape, axis):
    return lax.broadcasted_iota(jnp.int32, shape, axis)


def column(row):
    n = row.shape[1]
    same = iota((n, n), 0) == iota((n, n), 1)
    return jnp.sum(jnp.where(same, row, jnp.zeros((), row.dtype)), axis=1, keepdims=True)


def norm_silu(values, gain):
    mean_square = jnp.sum(values * values, axis=0, keepdims=True) * (1.0 / values.shape[0])
    half = (values * gain) * (0.5 * lax.rsqrt(mean_square + EPS))
    return (half + half * jnp.tanh(half)).astype(jnp.bfloat16)


def dot(a, b):
    return jnp.dot(a, b, preferred_element_type=jnp.float32)


def kernel(*refs):
    sources, (out_ref, *rest) = refs[:17], refs[17:]
    loaded, rest = rest[:17], rest[17:]
    (windows, w2, wd, heads, gin_s, gdown_s, bdown_s, parts, flags, enc, held, pick_s) = rest[:12]
    convolved, full, reduced = rest[12:15]
    load_sem, send_sem, recv_sem = rest[15:]
    loads = [
        pltpu.make_async_copy(source, target, load_sem.at[at])
        for at, (source, target) in enumerate(zip(sources, loaded))
    ]
    for load in loads:
        load.start()
    (
        lens_ref, readers_ref, owners_ref, frames_ref, wtab_ref, win_ref, bin_ref, gin_ref,
        wdown_ref, bdown_ref, gdown_ref, whead_ref, bhead_ref, etab_ref, dtab_ref, htab_ref,
        ptab_ref,
    ) = loaded
    me = lax.axis_index("wide")
    n, rows = held.shape[0], held.shape[1]
    barrier = pltpu.get_barrier_semaphore()
    for d in range(1, n):
        pl.semaphore_signal(
            barrier, inc=1, device_id={"wide": lax.rem(me + d, n)}, device_id_type=MESH
        )
    for load in loads[:4]:
        load.wait()
    read_rows = frames_ref.shape[0]
    most = read_rows // 4
    clips = lens_ref.shape[1]
    mine_at = me.astype(jnp.float32)
    len_row, reader_row, owner_row = (
        ref[...].astype(jnp.float32) for ref in (lens_ref, readers_ref, owners_ref)
    )
    len_col, reader_col, owner_col = column(len_row), column(reader_row), column(owner_row)
    earlier = iota((clips, clips), 1) < iota((clips, clips), 0)
    before_here = jnp.sum(
        jnp.where(earlier & (reader_row == reader_col), len_row, 0.0), axis=1, keepdims=True
    )
    first_len = jnp.sum(
        jnp.where((reader_col == mine_at) & (before_here == 0.0), len_col, 0.0),
        axis=0,
        keepdims=True,
    )

    last = 4 * most - 6
    row = iota((read_rows, 1), 0)
    number = ((row + 2) // 4 - 1).astype(jnp.float32)
    offset = ((row + 2) % 4).astype(jnp.float32)
    second = jnp.where(number >= first_len - 1.0, 1.0, 0.0)
    step = number + 1.0 - second * (first_len - 1.0)
    second_at = 4.0 * first_len - 3.0
    source = second * second_at + 4.0 * step - 3.0 + offset
    source = jnp.where(row < last, source, -1.0)
    source = jnp.where(row == 0, -1.0, source)
    source = jnp.where(row == 1, 0.0, source)
    source = jnp.where(row == last + 1, second_at, source)
    order = (iota((read_rows, read_rows), 1).astype(jnp.float32) == source).astype(jnp.bfloat16)
    frames = dot(order, frames_ref[...]).astype(jnp.bfloat16)
    flags[...] = jnp.where(
        iota(flags.shape, 0).astype(jnp.float32) == first_len - 1.0, 1.0, 0.0
    ) * jnp.ones(flags.shape, jnp.float32)

    stacked = jnp.concatenate(
        [
            frames[:, k * 1024 + h * 512 : k * 1024 + (h + 1) * 512]
            for k in range(3)
            for h in range(2)
        ],
        axis=0,
    )
    loads[4].wait()
    planes = dot(stacked, wtab_ref[...])
    lane = iota((read_rows, HALF), 1)
    for k in range(3):
        for dx in range(4):
            plane = []
            for py in range(2):
                at = (py * 4 + dx) * 128
                plane.append(
                    jnp.concatenate(
                        [
                            planes[
                                (2 * k + h) * read_rows : (2 * k + h + 1) * read_rows,
                                at : at + 128,
                            ]
                            for h in range(2)
                        ],
                        axis=1,
                    )
                )
            above = jnp.where(lane < 16, 0.0, pltpu.roll(plane[1], 16, 1))
            below = jnp.where(lane >= HALF - 16, 0.0, pltpu.roll(plane[0], HALF - 16, 1))
            for dy, value in enumerate((above, plane[0], plane[1], below)):
                row = (dy * 4 + dx) * 3 + k
                for h in range(2):
                    windows[h, pl.ds(row, read_rows, stride=PITCH), :] = value[
                        :, h * 128 : (h + 1) * 128
                    ]

    for load in loads[5:]:
        load.wait()
    spread = lax.dot_general(
        win_ref[...], etab_ref[...], (((0,), (0,)), ((), ())), preferred_element_type=jnp.float32
    )
    bias = column(bin_ref[...])
    high = bias.astype(jnp.bfloat16).astype(jnp.float32)
    mid = (bias - high).astype(jnp.bfloat16).astype(jnp.float32)
    low = bias - high - mid
    kcol = iota((128, KDIM), 1)
    tail = jnp.where(kcol == 3 * WIN, high, 0.0)
    tail = tail + jnp.where(kcol == 3 * WIN + 1, mid, 0.0)
    tail = tail + jnp.where(kcol == 3 * WIN + 2, low, 0.0)
    for ab in range(4):
        w2[ab * 128 : (ab + 1) * 128, :] = (
            spread[:, ab * 256 : ab * 256 + KDIM] + tail
        ).astype(jnp.bfloat16)
    wd[...] = dot(wdown_ref[...], dtab_ref[...]).astype(jnp.bfloat16)
    gin_s[...] = jnp.broadcast_to(column(gin_ref[...]), gin_s.shape)
    gdown_s[...] = jnp.broadcast_to(column(gdown_ref[...]), gdown_s.shape)
    bdown_s[...] = jnp.broadcast_to(column(bdown_ref[...]), bdown_s.shape)

    chunks = jnp.concatenate(
        [whead_ref[:, (s * 8 + c) * 256 : (s * 8 + c + 1) * 256] for c in range(8) for s in range(4)],
        axis=0,
    )
    turned = dot(chunks, htab_ref[...])
    piece = iota((64, 128), 1) // 16
    for ab in range(16):
        at = ab // 8 * 128
        row = jnp.zeros((64, 128), jnp.float32)
        for c in range(8):
            value = turned[c * 64 : (c + 1) * 64, at : at + 128]
            shift = (16 * c - ab % 8 * 16) % 128
            value = pltpu.roll(value, shift, 1) if shift else value
            row = jnp.where(piece == c, value, row)
        row = row.astype(jnp.bfloat16)
        for s in range(4):
            heads[ab * 16 : (ab + 1) * 16, s * 128 : (s + 1) * 128] = row[s * 16 : (s + 1) * 16]

    own_off = jnp.sum(
        jnp.where(earlier & (owner_row == owner_col), len_row, 0.0), axis=1, keepdims=True
    )
    slot = iota((clips, 128), 1).astype(jnp.float32)
    place = slot - own_off
    inside = (owner_col == mine_at) & (place >= 0.0) & (place < len_col)
    late = before_here > 0.0
    opening = jnp.where(late, 1.0, 0.0)
    later = jnp.where(late, before_here, 1.0) + place
    source = reader_col * rows + jnp.where(place == 0.0, opening, later)
    picked = jnp.sum(jnp.where(inside, source + 1.0, 0.0), axis=0, keepdims=True) - 1.0
    pick = (iota((n * rows, 128), 0).astype(jnp.float32) == picked).astype(jnp.float32)
    pick_s[...] = pick.T.astype(jnp.bfloat16)

    ones = jnp.ones((KDIM - 3 * WIN, HALF), jnp.bfloat16)

    def window(slot):
        return jnp.concatenate(
            [windows[h, pl.ds(slot * PITCH, WIN), :] for h in range(2)], axis=1
        )

    def stage(cols, odd, spot):
        if cols is not None:
            convolved[odd] = dot(w2[...], jnp.concatenate([cols, ones], axis=0))
        for row in range(0, 512, 128):
            full[1 - odd, row : row + 128, :] = norm_silu(
                convolved[1 - odd, row : row + 128, :], gin_s[...]
            )
        if spot is not None:
            second_product(odd, spot)

    def second_product(odd, spot):
        lowered = dot(wd[...], full[odd]) + bdown_s[...]
        reduced[spot * 128 : (spot + 1) * 128, :] = norm_silu(lowered, gdown_s[...])

    pix = iota((16, HALF), 1)
    sub = ((pix // 16) % 4) * 4 + pix % 4

    def keep(spot, both):
        total = jnp.zeros((16, HALF), jnp.float32)
        for ab in range(16):
            total = total + jnp.where(sub == ab, both[ab * 16 : (ab + 1) * 16, :], 0.0)
        parts[pl.ds(pl.multiple_of(spot * 16, 16), 16), :] = total

    def opening(at):
        blank = jnp.zeros((2 * WIN, HALF), jnp.bfloat16)
        return jnp.concatenate([blank, window(at).astype(jnp.bfloat16)], axis=0)

    def group_columns(at):
        flag = flags[pl.ds(at, 1), :]
        slots = [
            window(4 * at + s) * (1.0 - flag) + window(last + s) * flag for s in range(2)
        ]
        slots += [window(4 * at + s) for s in range(2, 6)]
        cols = jnp.concatenate(slots, axis=0).astype(jnp.bfloat16)
        return [cols[s * WIN : (s + 3) * WIN, :] for s in range(4)]

    first = jnp.concatenate([opening(1), ones], axis=0)
    convolved[0] = dot(w2[...], first)
    stage(opening(last + 1), 1, None)
    cols = group_columns(0)
    stage(cols[0], 0, 2)
    keep(0, dot(heads[:, 384:512], reduced[256:384, :]))
    stage(cols[1], 1, 3)
    keep(1, dot(heads[:, 384:512], reduced[384:512, :]))
    stage(cols[2], 0, 0)
    stage(cols[3], 1, 1)

    def group(at, carry):
        cols = group_columns(at)
        stage(cols[0], 0, 2)
        stage(cols[1], 1, 3)
        keep(at + 1, dot(heads[...], reduced[...]))
        stage(cols[2], 0, 0)
        stage(cols[3], 1, 1)
        return carry

    def pair(at, carry):
        group(2 * at + 1, carry)
        return group(2 * at + 2, carry)

    lax.fori_loop(0, (most - 3) // 2, pair, 0)
    if most % 2 == 0:
        group(most - 3, 0)
    stage(None, 0, 2)
    second_product(1, 3)
    keep(most - 1, dot(heads[...], reduced[...]))

    value = parts[...]
    top = value.astype(jnp.bfloat16)
    rest = (value - top.astype(jnp.float32)).astype(jnp.bfloat16)
    wide = dot(top, ptab_ref[...]) + dot(rest, ptab_ref[...])
    match = iota((most * 16, 256), 1) // 16 == iota((most * 16, 256), 0) % 16
    wide = jnp.where(match, wide, 0.0).reshape(most, 16, 256)
    bh = jnp.where(
        iota((16, 256), 1) // 16 == iota((16, 256), 0), column(bhead_ref[...]), 0.0
    )
    bh = jnp.sum(bh, axis=0, keepdims=True)
    result = jnp.sum(wide, axis=1) + bh
    if rows > most:
        result = jnp.concatenate([result, jnp.zeros((rows - most, 256), jnp.float32)], axis=0)
    enc[...] = result.astype(jnp.bfloat16)

    pl.semaphore_wait(barrier, n - 1)
    copies = []
    for d in range(1, n):
        copy = pltpu.make_async_remote_copy(
            src_ref=enc,
            dst_ref=held.at[me],
            send_sem=send_sem.at[d],
            recv_sem=recv_sem.at[d],
            device_id={"wide": lax.rem(me + d, n)},
            device_id_type=MESH,
        )
        copy.start()
        copies.append(copy)
    held[me] = enc[...]
    for copy in copies:
        copy.wait()
    result = dot(pick_s[...], held[...].reshape(n * rows, 256))
    out_ref[...] = result[: out_ref.shape[0]]


def shards(
    frames, latent_len, reader, owner, w_in, b_in, g_in, w_down, b_down, g_down, w_head, b_head
):
    n = lax.axis_size("wide")
    read_rows = frames.shape[0]
    most = read_rows // 4
    held_rows = -(-most // 16) * 16
    own_rows = 2 * ((most + 2) // 2)
    hbm = pl.BlockSpec(memory_space=pltpu.HBM)
    vmem = pl.BlockSpec(memory_space=pltpu.VMEM)
    wtab, etab, dtab, htab, ptab = (
        jnp.asarray(t, dtype=jnp.bfloat16)
        for t in (window_table(), weight_table(), down_table(), head_table(), place_table())
    )
    operands = (
        latent_len[None, :], reader[None, :], owner[None, :], frames, wtab, w_in.T,
        b_in[None, :], g_in[None, :], w_down, b_down[None, :], g_down[None, :], w_head,
        b_head[None, :], etab, dtab, htab, ptab,
    )
    picked = pl.pallas_call(
        kernel,
        out_shape=jax.ShapeDtypeStruct((-(-own_rows // 8) * 8, 256), jnp.float32),
        in_specs=[hbm] * len(operands),
        out_specs=vmem,
        scratch_shapes=[pltpu.VMEM(value.shape, value.dtype) for value in operands]
        + [
            pltpu.VMEM((2, read_rows * PITCH, 128), jnp.float32),
            pltpu.VMEM((512, KDIM), jnp.bfloat16),
            pltpu.VMEM((128, 512), jnp.bfloat16),
            pltpu.VMEM((256, 512), jnp.bfloat16),
            pltpu.VMEM((128, HALF), jnp.float32),
            pltpu.VMEM((128, HALF), jnp.float32),
            pltpu.VMEM((128, HALF), jnp.float32),
            pltpu.VMEM((most * 16, HALF), jnp.float32),
            pltpu.VMEM((most, HALF), jnp.float32),
            pltpu.VMEM((held_rows, 256), jnp.bfloat16),
            pltpu.VMEM((n, held_rows, 256), jnp.bfloat16),
            pltpu.VMEM((128, n * held_rows), jnp.bfloat16),
            pltpu.VMEM((2, 512, HALF), jnp.float32),
            pltpu.VMEM((2, 512, HALF), jnp.bfloat16),
            pltpu.VMEM((512, HALF), jnp.bfloat16),
            pltpu.SemaphoreType.DMA((len(operands),)),
            pltpu.SemaphoreType.DMA((n,)),
            pltpu.SemaphoreType.DMA((n,)),
        ],
        compiler_params=pltpu.CompilerParams(
            collective_id=0, has_side_effects=True, vmem_limit_bytes=56 * 1024 * 1024
        ),
        name="encode",
    )(*operands)
    return picked[:own_rows].astype(jnp.bfloat16)


def solution(mesh):
    return jax.shard_map(
        shards,
        mesh=mesh,
        in_specs=(
            P(("groups", "wide"), None),
            P("groups"),
            P("groups"),
            P("groups"),
            P(),
            P(),
            P(),
            P(),
            P(),
            P(),
            P(),
            P(),
        ),
        out_specs=P(("groups", "wide"), None),
        check_vma=False,
    )
```
